256 devices in a mesh: level: 16 (over x_lo, y, core), slab: 16 (over x_hi, z).
Axes of the slice: x: 4 (x_hi: 2, x_lo: 2; x = x_hi * 2 + x_lo), y: 4, z: 8, core: 2. Of those that a mesh axis runs over, the one named last changes fastest.
Arguments:
- right_side: float32 [64, 256, 512], P('slab', 'level'), may hold values from -6 to 6
- scale_field: float32 [64, 256, 512], P('slab', 'level'), may hold values from 0.7 to 1.4
- mass_field: float32 [64, 256, 512], P('slab', 'level'), may hold values from 0.05 to 0.5
- degrees: int32 [3], replicated, may hold values from 2 to 6, as said below
- lower_bound: float32 [3], replicated, may hold values from 0.05 to 0.3
- upper_bound: float32 [3], replicated, may hold values from 2 to 2.6
Outputs:
- solution: float32 [64, 256, 512], P('slab', 'level')
- final_res: float32 [64, 256, 512], P('slab', 'level')
The draws below stay inside these ranges and needn't reach their ends.
Inputs may be any that keep to these rules, and one draw needn't show every extreme that they name: `degrees`: degree of each grid; in every draw at least one grid has degree exactly 6.
All inputs are finite; a program needn't handle non-finite values.
Results may differ from the reference program's by a relative error of at most 0.0001.
Values sent between devices are 32-bit elements; how exact they have to be, the bound alone decides.
A program may use at most 128 MiB of HBM per device.

```python
import math
import jax
import jax.numpy as jnp

NY = 512
GRIDS = 3
CYCLES = 3
MAXDEG = 6
NZ = 64
NX = 256


def draw_degrees(key, part):
    first_key, second_key = jax.random.split(jax.random.fold_in(key, 17))
    values = jax.random.randint(first_key, (GRIDS,), 2, MAXDEG + 1)
    chosen = jax.random.randint(second_key, (), 0, GRIDS)
    return jnp.where(jnp.arange(GRIDS) == chosen, MAXDEG, values).astype(jnp.int32)


def levels(key, extent, shards, least, largest):
    level, own = 1.0, jax.random.fold_in(key, 6)
    for axis_at, parts in shards:
        steps = jnp.exp(jax.random.uniform(jax.random.fold_in(own, axis_at), (parts,), jnp.float32, least / len(shards), largest / len(shards)))
        level = level * jnp.repeat(steps, extent[axis_at] // parts).reshape([-1 if axis == axis_at else 1 for axis in range(len(extent))])
    return level


def bell_draw(key, dims, scale, limit, pieces=(), held_as=jnp.bfloat16):
    level = levels(key, dims, pieces, -0.22, 0.18) if pieces else 1.0
    result = jax.random.normal(key, dims, jnp.float32) * scale * level
    return jnp.minimum(jnp.maximum(result, -limit), limit).astype(held_as)


def setup_inputs(seed: int = 0) -> dict:
    seeds = jax.random.split(jax.random.key(seed), 7)
    right_side = bell_draw(seeds[0], (NZ, NX, NY), 1.0, 6.0, ((0, 16), (1, 16)), jnp.float32)
    scale_field = jnp.clip(jnp.exp(math.log(1.4) - 0.6931472 * jax.random.uniform(seeds[1], (NZ, NX, NY), jnp.float32) ** levels(seeds[1], (NZ, NX, NY), ((0, 16), (1, 16)), -0.2, 0.2)), 0.7, 1.4)
    mass_field = jnp.clip(jnp.exp(math.log(0.5) - 2.3025851 * jax.random.uniform(seeds[2], (NZ, NX, NY), jnp.float32) ** levels(seeds[2], (NZ, NX, NY), ((0, 16), (1, 16)), -0.2, 0.2)), 0.05, 0.5)
    degrees = draw_degrees(jax.random.fold_in(seeds[6], 71), 0)
    lower_bound = jnp.clip(jax.random.uniform(seeds[4], (GRIDS,), jnp.float32, 0.05, 0.3), 0.05, 0.3)
    upper_bound = jnp.clip(jax.random.uniform(seeds[5], (GRIDS,), jnp.float32, 2.0, 2.6), 2.0, 2.6)
    return dict(right_side=right_side, scale_field=scale_field, mass_field=mass_field, degrees=degrees, lower_bound=lower_bound, upper_bound=upper_bound)


def box_sum(padded):
    summed = padded[:-2] + padded[1:-1] + padded[2:]
    summed = summed[:, :-2] + summed[:, 1:-1] + summed[:, 2:]
    return summed[:, :, :-2] + summed[:, :, 1:-1] + summed[:, :, 2:]


def operate(field, coeff, mass_term):
    weighted = coeff * field
    padded = jnp.pad(weighted, 1)
    return coeff * ((27.0 / 26.0) * weighted - box_sum(padded) / 26.0) + mass_term * field


def average_cells(field):
    size_z, size_x, size_y = field.shape
    blocks = field.reshape(size_z // 2, 2, size_x // 2, 2, size_y // 2, 2)
    return jnp.mean(blocks, axis=(1, 3, 5))


def prolong(field):
    size_z, size_x, size_y = field.shape
    spread_out = jnp.broadcast_to(field[:, None, :, None, :, None], (size_z, 2, size_x, 2, size_y, 2))
    return spread_out.reshape(2 * size_z, 2 * size_x, 2 * size_y)


def smooth(source, coeff, mass_term, degree, bound_low, bound_high):
    inverse = 1.0 / (coeff * coeff + mass_term)
    centre = (bound_high + bound_low) * 0.5
    radius = (bound_high - bound_low) * 0.5
    spread_ratio = centre / radius
    direction = inverse * source / centre
    approx = direction
    rho_now = 1.0 / spread_ratio
    for step_no in range(1, MAXDEG):
        defect = source - operate(approx, coeff, mass_term)
        rho_new = 1.0 / (2.0 * spread_ratio - rho_now)
        new_dir = rho_new * rho_now * direction + (2.0 * rho_new / radius) * inverse * defect
        active = step_no < degree
        approx = jnp.where(active, approx + new_dir, approx)
        direction = jnp.where(active, new_dir, direction)
        rho_now = jnp.where(active, rho_new, rho_now)
    return approx


def reference(right_side, scale_field, mass_field, degrees, lower_bound, upper_bound):
    scale_mid = average_cells(scale_field)
    mass_mid = average_cells(mass_field)
    scale_low = average_cells(scale_mid)
    mass_low = average_cells(mass_mid)
    solution = jnp.zeros_like(right_side)
    for cycle_no in range(CYCLES):
        if cycle_no == 0:
            resid = right_side
        else:
            resid = right_side - operate(solution, scale_field, mass_field)
        resid_mid = 4.0 * average_cells(resid)
        resid_low = 4.0 * average_cells(resid_mid)
        fine_corr = smooth(resid, scale_field, mass_field, degrees[0], lower_bound[0], upper_bound[0])
        mid_corr = smooth(resid_mid, scale_mid, mass_mid, degrees[1], lower_bound[1], upper_bound[1])
        low_corr = smooth(resid_low, scale_low, mass_low, degrees[2], lower_bound[2], upper_bound[2])
        solution = solution + 0.5 * (fine_corr + prolong(mid_corr + prolong(low_corr)))
    final_res = right_side - operate(solution, scale_field, mass_field)
    return solution, final_res
```

```python
import jax
import jax.numpy as jnp
from jax import lax
from jax.experimental import pallas as pl
from jax.experimental.pallas import tpu as pltpu
from jax.sharding import PartitionSpec as P

CYCLES = 3
MAXDEG = 6
DEPTH = 6
PEERS = 16
LANES = 128
MESH = pl.DeviceIdType.MESH
f32 = jnp.float32


def split_matrices():
    row = lax.broadcasted_iota(jnp.int32, (LANES, LANES), 0)
    col = lax.broadcasted_iota(jnp.int32, (LANES, LANES), 1)
    spread = [jnp.where(row == half * 64 + col // 2, 1.0, 0.0).astype(f32) for half in (0, 1)]
    gather = [jnp.where(col == half * 64 + row // 2, 1.0, 0.0).astype(f32) for half in (0, 1)]
    return spread, gather


def dot(a, b):
    return jnp.dot(a, b, preferred_element_type=f32, precision=lax.Precision.HIGHEST)


def kernel(
    rhs, scale, mass, degrees, lower, upper, sol_out, res_out,
    gf, kf, cf, wf, df, sf, pf, jf, tmp_c, tmp_q, tmp_r,
    gm, km, im, wm, dm, em, pm, jm, mid_c, mid_q, mid_r,
    lb, gl, kl, il, wl, dl, el, jl,
    coef, send_sem, recv_sem,
):
    s = lax.axis_index("slab")
    l = lax.axis_index("level")
    count = [0]
    pending = []

    for ref in (gf.at[0], gf.at[1], gf.at[2], kf, cf, wf.at[0], wf.at[1],
                gm.at[0], gm.at[1], gm.at[2], km, im, wm.at[0], wm.at[1],
                gl, kl, il, wl.at[0], wl.at[1], el, em):
        def clear(z, carry, ref=ref):
            ref[z] = jnp.zeros(ref.shape[1:], f32)
            return carry
        lax.fori_loop(0, ref.shape[0], clear, 0)
    for kind in range(5):
        def clear_blocks(z, carry, kind=kind):
            lb[kind, z] = jnp.zeros((5, 4, LANES), f32)
            return carry
        lax.fori_loop(0, 13, clear_blocks, 0)

    barrier = pltpu.get_barrier_semaphore()
    for step in range(1, 7):
        for sign in (1, -1):
            @pl.when((s + sign * step >= 0) & (s + sign * step < PEERS))
            def _(step=step, sign=sign):
                pl.semaphore_signal(barrier, inc=1, device_id={"slab": s + sign * step, "level": l}, device_id_type=MESH)
    for step in range(1, 3):
        for sign in (1, -1):
            @pl.when((l + sign * step >= 0) & (l + sign * step < PEERS))
            def _(step=step, sign=sign):
                pl.semaphore_signal(barrier, inc=1, device_id={"slab": s, "level": l + sign * step}, device_id_type=MESH)

    class Message:
        def __init__(self, src, dst, ds=0, dl=0):
            self.at = count[0]
            count[0] += 1
            self.src, self.dst, self.ds, self.dl = src, dst, ds, dl
            pending.append(self)

        def copy(self):
            return pltpu.make_async_remote_copy(
                src_ref=self.src, dst_ref=self.dst,
                send_sem=send_sem.at[self.at], recv_sem=recv_sem.at[self.at],
                device_id={"slab": s + self.ds, "level": l + self.dl}, device_id_type=MESH,
            )

        def valid(self, sign):
            at, step = (s, self.ds) if self.ds else (l, self.dl)
            return (at + sign * step >= 0) & (at + sign * step < PEERS)

        def start(self):
            @pl.when(self.valid(1))
            def _():
                self.copy().start()

        def arrived(self):
            @pl.when(self.valid(-1))
            def _():
                self.copy().wait_recv()

        def sent(self):
            @pl.when(self.valid(1))
            def _():
                self.copy().wait_send()

    def start(messages):
        for m in messages:
            m.start()
        return messages

    def arrived(messages):
        for m in messages:
            m.arrived()

    def z_messages(view, own, depth, hop):
        layers = max(0, min(own, depth - own * (hop - 1)))
        if layers == 0:
            return []
        gap = own * (hop - 1)
        top, bottom = 6 + own, 6
        return [
            Message(view(top - layers, layers), view(6 - gap - layers, layers), ds=hop),
            Message(view(bottom, layers), view(top + gap, layers), ds=-hop),
        ]

    def x_messages(buf, first, planes, width):
        cut = lambda row: buf.at[pl.ds(first, planes), :, pl.ds(row, 8), :]
        return [
            Message(cut(16 + width - 8), cut(8), dl=1),
            Message(cut(16), cut(16 + width), dl=-1),
        ]

    def low_x_messages(kind, depth):
        cut = lambda block: lb.at[kind, pl.ds(6 - depth, 1 + 2 * depth), block]
        return [Message(cut(2), cut(2 - step), dl=step) for step in (1, -1, 2, -2)]

    fine_view = lambda buf: (lambda first, layers: buf.at[pl.ds(first, layers), :, pl.ds(16, 16), :])
    mid_view = lambda buf: (lambda first, layers: buf.at[pl.ds(first, layers), :, pl.ds(16, 8), :])
    low_view = lambda kind: (lambda first, layers: lb.at[kind, pl.ds(first, layers), 2])

    for grid in range(3):
        low_b = jnp.full((8, LANES), lower[grid], f32)
        high_b = jnp.full((8, LANES), upper[grid], f32)
        degree = jnp.full((8, LANES), degrees[grid], jnp.int32)
        centre = (high_b + low_b) * 0.5
        radius = (high_b - low_b) * 0.5
        ratio = centre / radius
        rho = 1.0 / ratio
        coef[grid, 0, 0] = 1.0 / centre
        for j in range(1, MAXDEG):
            rho_new = 1.0 / (2.0 * ratio - rho)
            active = j < degree
            coef[grid, j, 0] = jnp.where(active, rho_new * rho, 0.0)
            coef[grid, j, 1] = jnp.where(active, 2.0 * rho_new / radius, 0.0)
            rho = rho_new

    spread, gather = split_matrices()
    lane = lax.broadcasted_iota(jnp.int32, (1, LANES), 1)

    def tile_rows(v, rows):
        return jnp.concatenate([v] * (rows // 8), axis=0) if rows > 8 else v

    def x_sum(ref, z, tiles, r0, rows):
        return tuple(
            ref[z, t, pl.ds(r0 - 1, rows), :] + ref[z, t, pl.ds(r0, rows), :] + ref[z, t, pl.ds(r0 + 1, rows), :]
            for t in range(tiles)
        )

    def y_sum(vals):
        right = [pltpu.roll(v, 1, 1) for v in vals]
        left = [pltpu.roll(v, LANES - 1, 1) for v in vals]
        out = []
        for t, v in enumerate(vals):
            before = right[t - 1] if t > 0 else 0.0
            after = left[t + 1] if t + 1 < len(vals) else 0.0
            out.append(v + jnp.where(lane == 0, before, right[t]) + jnp.where(lane == LANES - 1, after, left[t]))
        return out

    def sweep(src, lo, hi, tiles, r0, rows, use):
        first = (x_sum(src, lo - 1, tiles, r0, rows), x_sum(src, lo, tiles, r0, rows))

        def plane(z, carry):
            below, here = carry
            above = x_sum(src, z + 1, tiles, r0, rows)
            box = y_sum([a + b + c for a, b, c in zip(below, here, above)])
            use(z, box)
            return here, above

        unroll = 2 if (hi - lo) % 2 == 0 else 1
        lax.fori_loop(lo, hi, plane, first, unroll=unroll)

    def smooth(grid, g, k, w, d, own, tiles, chunks):
        planes = own + 2 * DEPTH
        for j in range(1, MAXDEG):
            new = w.at[(j - 1) % 2]
            old = g if j == 1 else w.at[j % 2]
            for r0, rows in chunks:
                a = tile_rows(coef[grid, j, 0], rows)
                b = tile_rows(coef[grid, j, 1], rows)
                first = tile_rows(coef[grid, 0, 0], rows)

                def use(z, box, j=j, r0=r0, rows=rows, a=a, b=b, first=first, new=new, old=old):
                    cut = pl.ds(r0, rows)
                    for t in range(tiles):
                        source = g[z, t, cut, :]
                        if j == 1:
                            here = source * first
                            total = box[t] * first
                            direction = here
                        else:
                            here = old[z, t, cut, :]
                            total = box[t]
                            direction = d[z, t, cut, :]
                        defect = (source - here) + k[z, t, cut, :] * (total - here)
                        direction = a * direction + b * defect
                        d[z, t, cut, :] = direction
                        new[z, t, cut, :] = here + direction

                sweep(old, j, planes - j, tiles, r0, rows, use)

    def restrict(src, planes, tiles, rows):
        result = []
        for z in range(planes // 2):
            sums = []
            for t in range(tiles):
                total = None
                for dz in (0, 1):
                    for dx in (0, 1):
                        part = src[2 * z + dz, t, pl.ds(dx, rows, stride=2), :]
                        total = part if total is None else total + part
                sums.append(total * 0.125)
            result.append([
                dot(sums[2 * o], gather[0]) + dot(sums[2 * o + 1], gather[1]) for o in range(tiles // 2)
            ])
        return result

    for z in range(4):
        for t in range(4):
            cut = pl.ds(t * LANES, LANES)
            c = scale[z, :, cut]
            q = mass[z, :, cut]
            diag = c * c + q
            inverse = 1.0 / diag
            tmp_c[z, t] = c
            tmp_q[z, t] = q
            jf[z, t] = diag / c
            b = rhs[z, :, cut]
            tmp_r[z, t] = b
            kf[6 + z, t, pl.ds(16, 16), :] = c * c * inverse * (1.0 / 26.0)
            cf[6 + z, t, pl.ds(16, 16), :] = c
            gf[0, 6 + z, t, pl.ds(16, 16), :] = c * inverse * b

    greet = jnp.minimum(s, 6) + jnp.minimum(PEERS - 1 - s, 6) + jnp.minimum(l, 2) + jnp.minimum(PEERS - 1 - l, 2)
    pl.semaphore_wait(barrier, greet)

    for cycle in range(CYCLES):
        first = cycle == 0
        fine = [(gf.at[cycle], DEPTH)] + ([(kf, DEPTH - 1)] if first else [])
        near, far, side = [], [], []
        for buf, depth in fine:
            near += z_messages(fine_view(buf), 4, depth, 1)
            side += x_messages(buf, 6, 4, 16)
            far += z_messages(fine_view(buf), 4, depth, 2)
        if first:
            near += z_messages(fine_view(cf), 4, 1, 1)
        start(near)
        start(side)

        if first:
            cs, qs = restrict(tmp_c, 4, 4, 8), restrict(tmp_q, 4, 4, 8)
            for z in range(2):
                for t in range(2):
                    c, q = cs[z][t], qs[z][t]
                    diag = c * c + q
                    mid_c[z, t] = c
                    mid_q[z, t] = q
                    jm[z, t] = c / diag
                    km[6 + z, t, pl.ds(16, 8), :] = c * c / diag * (1.0 / 26.0)
                    im[6 + z, t, pl.ds(16, 8), :] = 1.0 / c
            c, q = restrict(mid_c, 2, 2, 4)[0][0], restrict(mid_q, 2, 2, 4)[0][0]
            diag = c * c + q
            jl[...] = c / diag
            lb[3, 6, 2] = c * c / diag * (1.0 / 26.0)
            lb[4, 6, 2] = 1.0 / c
        rs = restrict(tmp_r, 4, 4, 8)
        for z in range(2):
            for t in range(2):
                r = 4.0 * rs[z][t]
                mid_r[z, t] = r
                gm[cycle, 6 + z, t, pl.ds(16, 8), :] = r * jm[z, t]
        lb[cycle, 6, 2] = 4.0 * restrict(mid_r, 2, 2, 4)[0][0] * jl[...]

        kinds = [(cycle, DEPTH)] + ([(3, DEPTH - 1), (4, 1)] if first else [])
        low_z = []
        for kind, depth in kinds:
            for hop in range(1, 7):
                low_z += z_messages(low_view(kind), 1, depth, hop)
        start(low_z)
        mids = [(gm.at[cycle], DEPTH)] + ([(km, DEPTH - 1), (im, 1)] if first else [])
        mid_z = []
        for buf, depth in mids:
            for hop in range(1, 4):
                mid_z += z_messages(mid_view(buf), 2, depth, hop)
        start(mid_z)
        start(far)

        arrived(near)
        for buf, depth in fine:
            side += start(x_messages(buf, 2, 4, 16) + x_messages(buf, 10, 4, 16))
        if first:
            side += start(x_messages(cf, 5, 6, 16))
        arrived(low_z)
        low_x = []
        for kind, depth in kinds:
            low_x += start(low_x_messages(kind, depth))
        arrived(mid_z)
        mid_x = []
        for buf, depth in mids:
            mid_x += start(x_messages(buf, 6 - depth, 2 + 2 * depth, 8))
        arrived(far)
        for buf, depth in fine:
            side += start(x_messages(buf, 6 - depth, depth - 4, 16) + x_messages(buf, 14, depth - 4, 16))

        arrived(low_x)
        for kind, depth in kinds:
            dst = {3: kl, 4: il}.get(kind, gl)
            for block in range(5):
                dst[:, 0, pl.ds(8 + 4 * block, 4), :] = lb[kind, :, block]
        smooth(2, gl, kl, wl, dl, 1, 1, [(8, 24)])
        for z in range(5, 8):
            el[z - 5, 0, pl.ds(8, 24), :] = wl[0, z, 0, pl.ds(8, 24), :] * il[z, 0, pl.ds(8, 24), :]
        for z in range(3):
            coarse = el[z, 0, pl.ds(12, 16), :]
            for t in range(2):
                wide = dot(coarse, spread[t])
                for dx in (0, 1):
                    pm[z, t, pl.ds(8 + dx, 16, stride=2), :] = wide

        arrived(mid_x)
        smooth(1, gm.at[cycle], km, wm, dm, 2, 2, [(8, 24)])
        for z in range(5, 9):
            for t in range(2):
                cut = pl.ds(8, 24)
                em[z - 5, t, cut, :] = wm[0, z, t, cut, :] * im[z, t, cut, :] + pm[(z - 6) // 2 + 1, t, cut, :]
        for z in range(4):
            for t in range(4):
                wide = dot(em[z, t // 2, pl.ds(12, 16), :], spread[t % 2])
                for dx in (0, 1):
                    pf[z, t, pl.ds(8 + dx, 16, stride=2), :] = wide

        arrived(side)
        smooth(0, gf.at[cycle], kf, wf, df, 4, 4, [(8, 16), (24, 16)])
        for z in range(5, 11):
            for t in range(4):
                cut = pl.ds(8, 32)
                step = 0.5 * (wf[0, z, t, cut, :] + cf[z, t, cut, :] * pf[(z - 6) // 2 + 1, t, cut, :])
                sf[z, t, cut, :] = step if first else sf[z, t, cut, :] + step

        def residual(z, box, last=cycle == CYCLES - 1, cycle=cycle):
            cut = pl.ds(16, 16)
            for t in range(4):
                here = sf[z, t, cut, :]
                scaled = gf[0, z, t, cut, :] - here + kf[z, t, cut, :] * (box[t] - here)
                plain = scaled * jf[z - 6, t]
                if last:
                    out = pl.ds(t * LANES, LANES)
                    sol_out[z - 6, :, out] = here / cf[z, t, cut, :]
                    res_out[z - 6, :, out] = plain
                else:
                    gf[cycle + 1, z, t, cut, :] = scaled
                    tmp_r[z - 6, t] = plain

        sweep(sf, 6, 10, 4, 16, 16, residual)

    for m in pending:
        m.sent()


MESSAGES = 192


def shards(right_side, scale_field, mass_field, degrees, lower_bound, upper_bound):
    vmem = lambda *dims: pltpu.VMEM(dims, f32)
    fine, mid, low = (16, 4, 48, LANES), (14, 2, 40, LANES), (13, 1, 40, LANES)
    block = jax.ShapeDtypeStruct(right_side.shape, f32)
    whole = pl.BlockSpec(memory_space=pltpu.VMEM)
    scalar = pl.BlockSpec(memory_space=pltpu.SMEM)
    return pl.pallas_call(
        kernel,
        out_shape=(block, block),
        in_specs=[whole] * 3 + [scalar] * 3,
        out_specs=(whole, whole),
        scratch_shapes=[
            vmem(3, *fine), vmem(*fine), vmem(*fine), vmem(2, *fine), vmem(*fine), vmem(*fine),
            vmem(4, 4, 48, LANES), vmem(4, 4, 16, LANES), vmem(4, 4, 16, LANES), vmem(4, 4, 16, LANES), vmem(4, 4, 16, LANES),
            vmem(3, *mid), vmem(*mid), vmem(*mid), vmem(2, *mid), vmem(*mid), vmem(4, 2, 40, LANES),
            vmem(3, 2, 40, LANES), vmem(2, 2, 8, LANES), vmem(2, 2, 8, LANES), vmem(2, 2, 8, LANES), vmem(2, 2, 8, LANES),
            vmem(5, 13, 5, 4, LANES), vmem(*low), vmem(*low), vmem(*low), vmem(2, *low), vmem(*low),
            vmem(3, 1, 40, LANES), vmem(4, LANES),
            vmem(3, MAXDEG, 2, 8, LANES),
            pltpu.SemaphoreType.DMA((MESSAGES,)), pltpu.SemaphoreType.DMA((MESSAGES,)),
        ],
        compiler_params=pltpu.CompilerParams(
            collective_id=0, has_side_effects=True, vmem_limit_bytes=56 * 1024 * 1024
        ),
    )(right_side, scale_field, mass_field, degrees, lower_bound, upper_bound)


def solution(mesh):
    cut = P("slab", "level", None)
    return jax.shard_map(
        shards, mesh=mesh, in_specs=(cut, cut, cut, P(), P(), P()), out_specs=(cut, cut), check_vma=False
    )
```

```python
import jax
import jax.numpy as jnp
from jax import lax
from jax.experimental import pallas as pl
from jax.experimental.pallas import tpu as pltpu
from jax.sharding import PartitionSpec as P

CYCLES = 3
MAXDEG = 6
DEPTH = 6
UNROLL = True
PEERS = 16
LANES = 128
MESH = pl.DeviceIdType.MESH
f32 = jnp.float32
bf16 = jnp.bfloat16


def split_matrices():
    row = lax.broadcasted_iota(jnp.int32, (LANES, LANES), 0)
    col = lax.broadcasted_iota(jnp.int32, (LANES, LANES), 1)
    spread = [jnp.where(row == half * 64 + col // 2, 1.0, 0.0) for half in (0, 1)]
    gather = [jnp.where(col == half * 64 + row // 2, 1.0, 0.0) for half in (0, 1)]
    return jnp.concatenate(spread, axis=1).astype(bf16), jnp.concatenate(gather, axis=0).astype(bf16)


def dot(a, chosen):
    total = None
    for part in range(3):
        piece = a.astype(bf16)
        a = a - piece.astype(f32)
        product = jnp.dot(piece, chosen, preferred_element_type=f32)
        total = product if total is None else total + product
    return total


def kernel(
    rhs, scale, mass, degrees, lower, upper, sol_out, res_out,
    gf, kf, cf, wf, df, sf, pf, jf, tmp_c, tmp_q, tmp_r,
    gm, km, im, wm, dm, pm, jm, mid_c, mid_q, mid_r,
    lb, gl, kl, il, wl, dl, jl,
    coef, send_sem, recv_sem, cycle_send, cycle_recv,
):
    s = lax.axis_index("slab")
    l = lax.axis_index("level")
    once, every = [], []

    def clear(refs, first, planes, rows):
        for ref in refs:
            for z in range(first, first + planes):
                for t in range(ref.shape[1]):
                    ref[z, t, pl.ds(*rows), :] = jnp.zeros((rows[1], LANES), f32)

    fine_refs = [gf.at[0], gf.at[1], gf.at[2], kf, cf]
    mid_refs = [gm.at[0], gm.at[1], gm.at[2], km, im]
    low_refs = [lb.at[kind] for kind in range(5)]

    @pl.when(s < 6)
    def _():
        clear(fine_refs, 0, 6, (8, 32))
        clear(mid_refs, 0, 6, (8, 24))
        clear(low_refs, 0, 6, (0, 4))

    @pl.when(s > 9)
    def _():
        clear(fine_refs, 10, 6, (8, 32))
        clear(mid_refs, 8, 6, (8, 24))
        clear(low_refs, 7, 6, (0, 4))

    @pl.when(l < 2)
    def _():
        clear(fine_refs, 0, 16, (8, 8))
        clear(mid_refs, 0, 14, (8, 8))
        clear([ref.at[:, pl.ds(0, 2)] for ref in low_refs], 0, 13, (0, 4))

    @pl.when(l > 13)
    def _():
        clear(fine_refs, 0, 16, (32, 8))
        clear(mid_refs, 0, 14, (24, 8))
        clear([ref.at[:, pl.ds(3, 2)] for ref in low_refs], 0, 13, (0, 4))

    barrier = pltpu.get_barrier_semaphore()
    for step in range(1, 7):
        for sign in (1, -1):
            @pl.when((s + sign * step >= 0) & (s + sign * step < PEERS))
            def _(step=step, sign=sign):
                pl.semaphore_signal(barrier, inc=1, device_id={"slab": s + sign * step, "level": l}, device_id_type=MESH)
    for step in range(1, 3):
        for sign in (1, -1):
            @pl.when((l + sign * step >= 0) & (l + sign * step < PEERS))
            def _(step=step, sign=sign):
                pl.semaphore_signal(barrier, inc=1, device_id={"slab": s, "level": l + sign * step}, device_id_type=MESH)

    for hop in (2, -2):
        for step in (1, -1):
            @pl.when((s + hop >= 0) & (s + hop < PEERS) & (l + step >= 0) & (l + step < PEERS))
            def _(hop=hop, step=step):
                pl.semaphore_signal(barrier, inc=1, device_id={"slab": s + hop, "level": l + step}, device_id_type=MESH)

    class Message:
        def __init__(self, src, dst, ds=0, dl=0, cycle=None):
            kept = once if cycle is None else every
            self.at = len(kept)
            kept.append(self)
            self.src, self.dst, self.ds, self.dl, self.cycle = src, dst, ds, dl, cycle

        def copy(self):
            if self.cycle is None:
                send, recv = send_sem.at[self.at], recv_sem.at[self.at]
            else:
                send, recv = cycle_send.at[self.cycle].at[self.at], cycle_recv.at[self.cycle].at[self.at]
            return pltpu.make_async_remote_copy(
                src_ref=self.src, dst_ref=self.dst, send_sem=send, recv_sem=recv,
                device_id={"slab": s + self.ds, "level": l + self.dl}, device_id_type=MESH,
            )

        def valid(self, sign):
            inside = []
            for at, step in ((s, sign * self.ds), (l, sign * self.dl)):
                if step > 0:
                    inside.append(at < PEERS - step)
                elif step < 0:
                    inside.append(at >= -step)
            return inside[0] & inside[1] if len(inside) == 2 else inside[0]

        def start(self):
            @pl.when(self.valid(1))
            def _():
                self.copy().start()

        def arrived(self):
            @pl.when(self.valid(-1))
            def _():
                self.copy().wait_recv()

        def sent(self):
            @pl.when(self.valid(1))
            def _():
                self.copy().wait_send()

    def start(messages):
        for m in messages:
            m.start()
        return messages

    def arrived(messages):
        for m in messages:
            m.arrived()

    def z_messages(view, own, depth, hop, cycle=None):
        layers = max(0, min(own, depth - own * (hop - 1)))
        if layers == 0:
            return []
        gap = own * (hop - 1)
        top, bottom = 6 + own, 6
        return [
            Message(view(top - layers, layers), view(6 - gap - layers, layers), ds=hop, cycle=cycle),
            Message(view(bottom, layers), view(top + gap, layers), ds=-hop, cycle=cycle),
        ]

    def far_messages(buf, layers, cycle=None):
        result = []
        for ds, src, dst in ((2, 10 - layers, 2 - layers), (-2, 6, 14)):
            for dl, row, to, rows in ((0, 16, 16, 16), (1, 24, 8, 8), (-1, 16, 32, 8)):
                cut = lambda first, at: buf.at[pl.ds(first, layers), :, pl.ds(at, rows), :]
                result.append(Message(cut(src, row), cut(dst, to), ds=ds, dl=dl, cycle=cycle))
        return result

    def x_messages(buf, first, planes, width, cycle=None):
        cut = lambda row: buf.at[pl.ds(first, planes), :, pl.ds(row, 8), :]
        return [
            Message(cut(16 + width - 8), cut(8), dl=1, cycle=cycle),
            Message(cut(16), cut(16 + width), dl=-1, cycle=cycle),
        ]

    def low_x_messages(kind, depth, cycle=None):
        cut = lambda block: lb.at[kind].at[pl.ds(6 - depth, 1 + 2 * depth), block]
        return [Message(cut(2), cut(2 - step), dl=step, cycle=cycle) for step in (1, -1, 2, -2)]

    fine_view = lambda buf: (lambda first, layers: buf.at[pl.ds(first, layers), :, pl.ds(16, 16), :])
    mid_view = lambda buf: (lambda first, layers: buf.at[pl.ds(first, layers), :, pl.ds(16, 8), :])
    low_view = lambda kind: (lambda first, layers: lb.at[kind].at[pl.ds(first, layers), 2])

    for grid in range(3):
        low_b = jnp.full((8, LANES), lower[grid], f32)
        high_b = jnp.full((8, LANES), upper[grid], f32)
        degree = jnp.full((8, LANES), degrees[grid], jnp.int32)
        centre = (high_b + low_b) * 0.5
        radius = (high_b - low_b) * 0.5
        ratio = centre / radius
        rho = 1.0 / ratio
        coef[grid, 0, 0] = 1.0 / centre
        for j in range(1, MAXDEG):
            rho_new = 1.0 / (2.0 * ratio - rho)
            active = j < degree
            coef[grid, j, 0] = jnp.where(active, rho_new * rho, 0.0)
            coef[grid, j, 1] = jnp.where(active, 2.0 * rho_new / radius, 0.0)
            rho = rho_new

    spread, gather = split_matrices()
    lane = lax.broadcasted_iota(jnp.int32, (1, LANES), 1)

    def tile_rows(v, rows):
        return jnp.concatenate([v] * (rows // 8), axis=0) if rows > 8 else v

    def x_sum(ref, z, tiles, r0, rows):
        return tuple(
            ref[z, t, pl.ds(r0 - 1, rows), :] + ref[z, t, pl.ds(r0, rows), :] + ref[z, t, pl.ds(r0 + 1, rows), :]
            for t in range(tiles)
        )

    def y_sum(vals):
        right = [pltpu.roll(v, 1, 1) for v in vals]
        left = [pltpu.roll(v, LANES - 1, 1) for v in vals]
        out = []
        for t, v in enumerate(vals):
            before = right[t - 1] if t > 0 else 0.0
            after = left[t + 1] if t + 1 < len(vals) else 0.0
            out.append(v + jnp.where(lane == 0, before, right[t]) + jnp.where(lane == LANES - 1, after, left[t]))
        return out

    def sweep(src, lo, hi, tiles, r0, rows, use, whole=True):
        first = (x_sum(src, lo - 1, tiles, r0, rows), x_sum(src, lo, tiles, r0, rows))

        def plane(z, carry):
            below, here = carry
            above = x_sum(src, z + 1, tiles, r0, rows)
            box = y_sum([a + b + c for a, b, c in zip(below, here, above)])
            use(z, box)
            return here, above

        if whole:
            carry = first
            for z in range(lo, hi):
                carry = plane(z, carry)
        else:
            lax.fori_loop(lo, hi, plane, first, unroll=(hi - lo) // 2)

    def smooth(grid, g, k, w, d, own, tiles, chunks):
        planes = own + 2 * DEPTH
        for j in range(1, MAXDEG):
            new = w.at[(j - 1) % 2]
            old = g if j == 1 else w.at[j % 2]
            for r0, rows in chunks:
                a = tile_rows(coef[grid, j, 0], rows)
                b = tile_rows(coef[grid, j, 1], rows)
                first = tile_rows(coef[grid, 0, 0], rows)

                def use(z, box, j=j, r0=r0, rows=rows, a=a, b=b, first=first, new=new, old=old):
                    cut = pl.ds(r0, rows)
                    for t in range(tiles):
                        source = g[z, t, cut, :]
                        if j == 1:
                            here = source * first
                            total = box[t] * first
                            direction = here
                        else:
                            here = old[z, t, cut, :]
                            total = box[t]
                            direction = d[z, t, cut, :]
                        defect = (source - here) + k[z, t, cut, :] * (total - here)
                        direction = a * direction + b * defect
                        d[z, t, cut, :] = direction
                        new[z, t, cut, :] = here + direction

                sweep(old, j, planes - j, tiles, r0, rows, use, whole=UNROLL or grid > 0)

    def restrict(src, planes, tiles, rows):
        sums = []
        for z in range(planes // 2):
            for t in range(tiles):
                total = None
                for dz in (0, 1):
                    for dx in (0, 1):
                        part = src[2 * z + dz, t, pl.ds(dx, rows, stride=2), :]
                        total = part if total is None else total + part
                sums.append(total * 0.125)
        pairs = [jnp.concatenate(sums[at:at + 2], axis=1) for at in range(0, len(sums), 2)]
        joined = dot(jnp.concatenate(pairs, axis=0), gather)
        half = tiles // 2
        return [
            [joined[rows * (z * half + o):rows * (z * half + o + 1)] for o in range(half)] for z in range(planes // 2)
        ]

    for z in range(4):
        for t in range(4):
            cut = pl.ds(t * LANES, LANES)
            c = scale[z, :, cut]
            q = mass[z, :, cut]
            diag = c * c + q
            inverse = 1.0 / diag
            tmp_c[z, t] = c
            tmp_q[z, t] = q
            jf[z, t] = diag / c
            b = rhs[z, :, cut]
            tmp_r[z, t] = b
            kf[6 + z, t, pl.ds(16, 16), :] = c * c * inverse * (1.0 / 26.0)
            cf[6 + z, t, pl.ds(16, 16), :] = c
            gf[0, 6 + z, t, pl.ds(16, 16), :] = c * inverse * b

    up, down = jnp.minimum(s, 6), jnp.minimum(PEERS - 1 - s, 6)
    left, right = jnp.minimum(l, 2), jnp.minimum(PEERS - 1 - l, 2)
    corners = (jnp.minimum(up // 2, 1) + jnp.minimum(down // 2, 1)) * (jnp.minimum(left, 1) + jnp.minimum(right, 1))
    greet = up + down + left + right + corners
    pl.semaphore_wait(barrier, greet)

    for z in range(5, 11):
        for t in range(4):
            sf[z, t, pl.ds(8, 32), :] = jnp.zeros((32, LANES), f32)

    shallow = DEPTH - 1
    near_k = z_messages(fine_view(kf), 4, shallow, 1) + z_messages(fine_view(cf), 4, 1, 1)
    side_k = x_messages(kf, 6, 4, 16)
    far_k = far_messages(kf, shallow - 4)
    low_zk, mid_zk = [], []
    for hop in range(1, 7):
        low_zk += z_messages(low_view(3), 1, shallow, hop) + z_messages(low_view(4), 1, 1, hop)
    for hop in range(1, 4):
        mid_zk += z_messages(mid_view(km), 2, shallow, hop) + z_messages(mid_view(im), 2, 1, hop)
    low_xk = low_x_messages(3, shallow) + low_x_messages(4, 1)
    mid_xk = x_messages(km, 1, 12, 8) + x_messages(im, 5, 4, 8)
    relay_k = x_messages(kf, 2, 4, 16) + x_messages(kf, 10, 4, 16) + x_messages(cf, 5, 6, 16)

    def cycle_body(cycle, carry):
        opening = pl.when(cycle == 0)
        g = gf.at[cycle]
        near = z_messages(fine_view(g), 4, DEPTH, 1, cycle)
        side = x_messages(g, 6, 4, 16, cycle)
        far = far_messages(g, DEPTH - 4, cycle)
        start(near)
        start(side)

        @opening
        def _():
            start(near_k)
            start(side_k)
            cs, qs = restrict(tmp_c, 4, 4, 8), restrict(tmp_q, 4, 4, 8)
            for z in range(2):
                for t in range(2):
                    c, q = cs[z][t], qs[z][t]
                    diag = c * c + q
                    mid_c[z, t] = c
                    mid_q[z, t] = q
                    jm[z, t] = c / diag
                    km[6 + z, t, pl.ds(16, 8), :] = c * c / diag * (1.0 / 26.0)
                    im[6 + z, t, pl.ds(16, 8), :] = 1.0 / c
            c, q = restrict(mid_c, 2, 2, 4)[0][0], restrict(mid_q, 2, 2, 4)[0][0]
            diag = c * c + q
            jl[...] = c / diag
            lb[3, 6, 2] = c * c / diag * (1.0 / 26.0)
            lb[4, 6, 2] = 1.0 / c

        rs = restrict(tmp_r, 4, 4, 8)
        for z in range(2):
            for t in range(2):
                r = 4.0 * rs[z][t]
                mid_r[z, t] = r
                gm[cycle, 6 + z, t, pl.ds(16, 8), :] = r * jm[z, t]
        lb[cycle, 6, 2] = 4.0 * restrict(mid_r, 2, 2, 4)[0][0] * jl[...]

        low_z, mid_z = [], []
        for hop in range(1, 7):
            low_z += z_messages(low_view(cycle), 1, DEPTH, hop, cycle)
        for hop in range(1, 4):
            mid_z += z_messages(mid_view(gm.at[cycle]), 2, DEPTH, hop, cycle)
        low_x = low_x_messages(cycle, DEPTH, cycle)
        mid_x = x_messages(gm.at[cycle], 0, 14, 8, cycle)
        relay = x_messages(g, 2, 4, 16, cycle) + x_messages(g, 10, 4, 16, cycle)
        start(low_z)
        start(mid_z)
        start(far)

        @opening
        def _():
            start(low_zk)
            start(mid_zk)
            start(far_k)

        arrived(near)
        start(relay)

        @opening
        def _():
            arrived(near_k)
            start(relay_k)

        arrived(low_z)
        start(low_x)
        arrived(mid_z)
        start(mid_x)

        @opening
        def _():
            arrived(low_zk)
            start(low_xk)
            arrived(mid_zk)
            start(mid_xk)

        arrived(low_x)

        @opening
        def _():
            arrived(low_xk)
            for kind, dst in ((3, kl), (4, il)):
                for block in range(5):
                    dst[:, 0, pl.ds(6 + 4 * block, 4), :] = lb[kind, :, block]

        for block in range(5):
            gl[:, 0, pl.ds(6 + 4 * block, 4), :] = lb[cycle, :, block]
        smooth(2, gl, kl, wl, dl, 1, 1, [(8, 16)])
        cut = pl.ds(12, 8)
        coarse = jnp.concatenate([wl[0, z, 0, cut, :] * il[z, 0, cut, :] for z in range(5, 8)], axis=0)
        wide = dot(coarse, spread)
        for z in range(3):
            for t in range(2):
                for dx in (0, 1):
                    pm[z, t, pl.ds(dx, 8, stride=2), :] = wide[8 * z:8 * z + 8, t * LANES:(t + 1) * LANES]

        arrived(mid_x)
        opening(lambda: arrived(mid_xk))
        smooth(1, gm.at[cycle], km, wm, dm, 2, 2, [(8, 24)])
        cut = pl.ds(12, 16)
        coarse = jnp.concatenate([
            wm[0, z, t, cut, :] * im[z, t, cut, :] + pm[(z - 6) // 2 + 1, t]
            for z in range(5, 9) for t in range(2)
        ], axis=0)
        wide = dot(coarse, spread)
        for z in range(4):
            for t in range(4):
                row, half = 16 * (2 * z + t // 2), t % 2
                for dx in (0, 1):
                    pf[z, t, pl.ds(dx, 16, stride=2), :] = wide[row:row + 16, half * LANES:(half + 1) * LANES]

        arrived(far)
        arrived(side + relay)
        opening(lambda: arrived(far_k + side_k + relay_k))
        smooth(0, g, kf, wf, df, 4, 4, [(8, 16), (24, 16)])
        for z in range(5, 11):
            for t in range(4):
                cut = pl.ds(8, 32)
                step = 0.5 * (wf[0, z, t, cut, :] + cf[z, t, cut, :] * pf[(z - 6) // 2 + 1, t])
                sf[z, t, cut, :] += step

        def residual(z, box):
            cut = pl.ds(16, 16)
            for t in range(4):
                here = sf[z, t, cut, :]
                scaled = gf[0, z, t, cut, :] - here + kf[z, t, cut, :] * (box[t] - here)
                plain = scaled * jf[z - 6, t]
                gf[cycle + 1, z, t, cut, :] = scaled
                tmp_r[z - 6, t] = plain
                out = pl.ds(t * LANES, LANES)
                sol_out[z - 6, :, out] = here / cf[z, t, cut, :]
                res_out[z - 6, :, out] = plain

        sweep(sf, 6, 10, 4, 16, 16, residual)
        for m in every:
            m.sent()
        return carry

    lax.fori_loop(0, CYCLES, cycle_body, 0)
    assert len(once) <= ONCE and len(every) <= EVERY
    for m in once:
        m.sent()


ONCE, EVERY = 80, 48


def shards(right_side, scale_field, mass_field, degrees, lower_bound, upper_bound):
    vmem = lambda *dims: pltpu.VMEM(dims, f32)
    fine, mid, low = (16, 4, 48, LANES), (14, 2, 40, LANES), (13, 1, 40, LANES)
    block = jax.ShapeDtypeStruct(right_side.shape, f32)
    whole = pl.BlockSpec(memory_space=pltpu.VMEM)
    scalar = pl.BlockSpec(memory_space=pltpu.SMEM)
    return pl.pallas_call(
        kernel,
        out_shape=(block, block),
        in_specs=[whole] * 3 + [scalar] * 3,
        out_specs=(whole, whole),
        scratch_shapes=[
            vmem(4, *fine), vmem(*fine), vmem(*fine), vmem(2, *fine), vmem(*fine), vmem(*fine),
            vmem(4, 4, 32, LANES), vmem(4, 4, 16, LANES), vmem(4, 4, 16, LANES), vmem(4, 4, 16, LANES), vmem(4, 4, 16, LANES),
            vmem(3, *mid), vmem(*mid), vmem(*mid), vmem(2, *mid), vmem(*mid),
            vmem(3, 2, 16, LANES), vmem(2, 2, 8, LANES), vmem(2, 2, 8, LANES), vmem(2, 2, 8, LANES), vmem(2, 2, 8, LANES),
            vmem(5, 13, 5, 4, LANES), vmem(*low), vmem(*low), vmem(*low), vmem(2, *low), vmem(*low),
            vmem(4, LANES),
            vmem(3, MAXDEG, 2, 8, LANES),
            pltpu.SemaphoreType.DMA((ONCE,)), pltpu.SemaphoreType.DMA((ONCE,)),
            pltpu.SemaphoreType.DMA((CYCLES, EVERY)), pltpu.SemaphoreType.DMA((CYCLES, EVERY)),
        ],
        compiler_params=pltpu.CompilerParams(
            collective_id=0, has_side_effects=True, vmem_limit_bytes=56 * 1024 * 1024
        ),
    )(right_side, scale_field, mass_field, degrees, lower_bound, upper_bound)


def solution(mesh):
    cut = P("slab", "level", None)
    return jax.shard_map(
        shards, mesh=mesh, in_specs=(cut, cut, cut, P(), P(), P()), out_specs=(cut, cut), check_vma=False
    )
```

```python
import jax
import jax.numpy as jnp
from jax import lax
from jax.experimental import pallas as pl
from jax.experimental.pallas import tpu as pltpu
from jax.sharding import PartitionSpec as P

CYCLES = 3
MAXDEG = 6
DEPTH = 6
PEERS = 16
LANES = 128
MESH = pl.DeviceIdType.MESH
f32 = jnp.float32
bf16 = jnp.bfloat16


def split_matrices():
    row = lax.broadcasted_iota(jnp.int32, (LANES, LANES), 0)
    col = lax.broadcasted_iota(jnp.int32, (LANES, LANES), 1)
    spread = [jnp.where(row == half * 64 + col // 2, 1.0, 0.0) for half in (0, 1)]
    gather = [jnp.where(col == half * 64 + row // 2, 1.0, 0.0) for half in (0, 1)]
    return jnp.concatenate(spread, axis=1).astype(bf16), jnp.concatenate(gather, axis=0).astype(bf16)


def dot(a, chosen):
    total = None
    for part in range(3):
        piece = a.astype(bf16)
        a = a - piece.astype(f32)
        product = jnp.dot(piece, chosen, preferred_element_type=f32)
        total = product if total is None else total + product
    return total


def kernel(
    rhs_in, scale_in, mass_in, degrees, lower, upper, sol_out, res_out,
    rhs, scale, mass,
    gf, kf, cf, wf, df, sf, pf, jf, tmp_c, tmp_q, tmp_r,
    gm, km, im, wm, dm, pm, jm, mid_c, mid_q, mid_r,
    lb, gl, kl, il, wl, dl, jl,
    coef, load_sem, send_sem, recv_sem, cycle_send, cycle_recv,
):
    s = lax.axis_index("slab")
    l = lax.axis_index("level")
    once, every = [], []
    loads = [
        pltpu.make_async_copy(src, dst, load_sem.at[i])
        for i, (src, dst) in enumerate(((scale_in, scale), (mass_in, mass), (rhs_in, rhs)))
    ]
    for load in loads:
        load.start()

    def clear(refs, first, planes, rows):
        for ref in refs:
            for z in range(first, first + planes):
                for t in range(ref.shape[1]):
                    ref[z, t, pl.ds(*rows), :] = jnp.zeros((rows[1], LANES), f32)

    fine_refs = [gf.at[0], gf.at[1], gf.at[2], kf, cf]
    mid_refs = [gm.at[0], gm.at[1], gm.at[2], km, im]
    low_refs = [lb.at[kind] for kind in range(5)]

    @pl.when(s < 6)
    def _():
        clear(fine_refs, 0, 6, (8, 32))
        clear(mid_refs, 0, 6, (8, 24))
        clear(low_refs, 0, 6, (0, 4))

    @pl.when(s > 9)
    def _():
        clear(fine_refs, 10, 6, (8, 32))
        clear(mid_refs, 8, 6, (8, 24))
        clear(low_refs, 7, 6, (0, 4))

    @pl.when(l < 2)
    def _():
        clear(fine_refs, 0, 16, (8, 8))
        clear(mid_refs, 0, 14, (8, 8))
        clear([ref.at[:, pl.ds(0, 2)] for ref in low_refs], 0, 13, (0, 4))

    @pl.when(l > 13)
    def _():
        clear(fine_refs, 0, 16, (32, 8))
        clear(mid_refs, 0, 14, (24, 8))
        clear([ref.at[:, pl.ds(3, 2)] for ref in low_refs], 0, 13, (0, 4))

    barrier = pltpu.get_barrier_semaphore()
    for step in range(1, 7):
        for sign in (1, -1):
            @pl.when((s + sign * step >= 0) & (s + sign * step < PEERS))
            def _(step=step, sign=sign):
                pl.semaphore_signal(barrier, inc=1, device_id={"slab": s + sign * step, "level": l}, device_id_type=MESH)
    for step in range(1, 3):
        for sign in (1, -1):
            @pl.when((l + sign * step >= 0) & (l + sign * step < PEERS))
            def _(step=step, sign=sign):
                pl.semaphore_signal(barrier, inc=1, device_id={"slab": s, "level": l + sign * step}, device_id_type=MESH)

    class Message:
        def __init__(self, src, dst, ds=0, dl=0, cycle=None):
            kept = once if cycle is None else every
            self.at = len(kept)
            kept.append(self)
            self.src, self.dst, self.ds, self.dl, self.cycle = src, dst, ds, dl, cycle

        def copy(self):
            if self.cycle is None:
                send, recv = send_sem.at[self.at], recv_sem.at[self.at]
            else:
                send, recv = cycle_send.at[self.cycle].at[self.at], cycle_recv.at[self.cycle].at[self.at]
            return pltpu.make_async_remote_copy(
                src_ref=self.src, dst_ref=self.dst, send_sem=send, recv_sem=recv,
                device_id={"slab": s + self.ds, "level": l + self.dl}, device_id_type=MESH,
            )

    def by_partner(messages, sign, act):
        groups = {}
        for m in messages:
            groups.setdefault((sign * m.ds, sign * m.dl), []).append(m)
        for (ds, dl), group in groups.items():
            at, step = (s, ds) if ds else (l, dl)

            @pl.when(at < PEERS - step if step > 0 else at >= -step)
            def _(group=group):
                for m in group:
                    act(m)

    def start(messages):
        by_partner(messages, 1, lambda m: m.copy().start())

    def arrived(messages):
        by_partner(messages, -1, lambda m: m.copy().wait_recv())

    def sent(messages):
        by_partner(messages, 1, lambda m: m.copy().wait_send())

    def z_messages(view, own, depth, hop, cycle=None):
        layers = max(0, min(own, depth - own * (hop - 1)))
        if layers == 0:
            return []
        gap = own * (hop - 1)
        top, bottom = 6 + own, 6
        return [
            Message(view(top - layers, layers), view(6 - gap - layers, layers), ds=hop, cycle=cycle),
            Message(view(bottom, layers), view(top + gap, layers), ds=-hop, cycle=cycle),
        ]

    def x_messages(buf, first, planes, width, cycle=None):
        cut = lambda row: buf.at[pl.ds(first, planes), :, pl.ds(row, 6), :]
        return [
            Message(cut(16 + width - 6), cut(10), dl=1, cycle=cycle),
            Message(cut(16), cut(16 + width), dl=-1, cycle=cycle),
        ]

    def low_x_messages(kind, depth, cycle=None):
        cut = lambda block: lb.at[kind].at[pl.ds(6 - depth, 1 + 2 * depth), block]
        return [Message(cut(2), cut(2 - step), dl=step, cycle=cycle) for step in (1, -1, 2, -2)]

    fine_view = lambda buf: (lambda first, layers: buf.at[pl.ds(first, layers), :, pl.ds(16, 16), :])
    mid_view = lambda buf: (lambda first, layers: buf.at[pl.ds(first, layers), :, pl.ds(16, 8), :])
    low_view = lambda kind: (lambda first, layers: lb.at[kind].at[pl.ds(first, layers), 2])

    for grid in range(3):
        low_b = jnp.full((8, LANES), lower[grid], f32)
        high_b = jnp.full((8, LANES), upper[grid], f32)
        degree = jnp.full((8, LANES), degrees[grid], jnp.int32)
        centre = (high_b + low_b) * 0.5
        radius = (high_b - low_b) * 0.5
        ratio = centre / radius
        rho = 1.0 / ratio
        coef[grid, 0, 0] = 1.0 / centre
        for j in range(1, MAXDEG):
            rho_new = 1.0 / (2.0 * ratio - rho)
            active = j < degree
            coef[grid, j, 0] = jnp.where(active, rho_new * rho, 0.0)
            coef[grid, j, 1] = jnp.where(active, 2.0 * rho_new / radius, 0.0)
            rho = rho_new

    spread, gather = split_matrices()
    lane = lax.broadcasted_iota(jnp.int32, (1, LANES), 1)

    def tile_rows(v, rows):
        return jnp.concatenate([v] * (rows // 8), axis=0) if rows > 8 else v

    def x_sum(ref, z, tiles, r0, rows):
        return tuple(
            ref[z, t, pl.ds(r0 - 1, rows), :] + ref[z, t, pl.ds(r0, rows), :] + ref[z, t, pl.ds(r0 + 1, rows), :]
            for t in range(tiles)
        )

    def y_sum(vals):
        right = [pltpu.roll(v, 1, 1) for v in vals]
        left = [pltpu.roll(v, LANES - 1, 1) for v in vals]
        out = []
        for t, v in enumerate(vals):
            before = right[t - 1] if t > 0 else 0.0
            after = left[t + 1] if t + 1 < len(vals) else 0.0
            out.append(v + jnp.where(lane == 0, before, right[t]) + jnp.where(lane == LANES - 1, after, left[t]))
        return out

    def sweep(src, lo, hi, tiles, r0, rows, use):
        first = (x_sum(src, lo - 1, tiles, r0, rows), x_sum(src, lo, tiles, r0, rows))

        def plane(z, carry):
            below, here = carry
            above = x_sum(src, z + 1, tiles, r0, rows)
            box = y_sum([a + b + c for a, b, c in zip(below, here, above)])
            use(z, box)
            return here, above

        for z in range(lo, hi):
            first = plane(z, first)

    def smooth(grid, g, k, w, d, own, tiles, chunks, spans=None):
        planes = own + 2 * DEPTH
        for j in range(1, MAXDEG):
            new, turn = w.at[j - 1], d.at[j - 1]
            old, past = (g, None) if j == 1 else (w.at[j - 2], d.at[j - 2])
            parts = [(j, planes - j)] if spans is None else spans(j)
            for (r0, rows), (lo, hi) in [(chunk, part) for chunk in chunks for part in parts]:
                a = tile_rows(coef[grid, j, 0], rows)
                b = tile_rows(coef[grid, j, 1], rows)
                first = tile_rows(coef[grid, 0, 0], rows)

                def use(z, box, j=j, r0=r0, rows=rows, a=a, b=b, first=first, new=new, old=old, turn=turn, past=past):
                    cut = pl.ds(r0, rows)
                    for t in range(tiles):
                        source = g[z, t, cut, :]
                        if j == 1:
                            here = source * first
                            total = box[t] * first
                            direction = here
                        else:
                            here = old[z, t, cut, :]
                            total = box[t]
                            direction = past[z, t, cut, :]
                        defect = (source - here) + k[z, t, cut, :] * (total - here)
                        direction = a * direction + b * defect
                        turn[z, t, cut, :] = direction
                        new[z, t, cut, :] = here + direction

                sweep(old, lo, hi, tiles, r0, rows, use)

    def restrict(src, planes, tiles, rows):
        sums = []
        for z in range(planes // 2):
            for t in range(tiles):
                total = None
                for dz in (0, 1):
                    for dx in (0, 1):
                        part = src[2 * z + dz, t, pl.ds(dx, rows, stride=2), :]
                        total = part if total is None else total + part
                sums.append(total * 0.125)
        pairs = [jnp.concatenate(sums[at:at + 2], axis=1) for at in range(0, len(sums), 2)]
        joined = dot(jnp.concatenate(pairs, axis=0), gather)
        half = tiles // 2
        return [
            [joined[rows * (z * half + o):rows * (z * half + o + 1)] for o in range(half)] for z in range(planes // 2)
        ]

    for load in loads:
        load.wait()
    for z in range(4):
        for t in range(4):
            cut = pl.ds(t * LANES, LANES)
            c = scale[z, :, cut]
            q = mass[z, :, cut]
            diag = c * c + q
            inverse = 1.0 / diag
            tmp_c[z, t] = c
            tmp_q[z, t] = q
            jf[z, t] = diag / c
            b = rhs[z, :, cut]
            tmp_r[z, t] = b
            kf[6 + z, t, pl.ds(16, 16), :] = c * c * inverse * (1.0 / 26.0)
            cf[6 + z, t, pl.ds(16, 16), :] = c
            gf[0, 6 + z, t, pl.ds(16, 16), :] = c * inverse * b

    up, down = jnp.minimum(s, 6), jnp.minimum(PEERS - 1 - s, 6)
    left, right = jnp.minimum(l, 2), jnp.minimum(PEERS - 1 - l, 2)
    pl.semaphore_wait(barrier, up + down + left + right)

    for z in range(5, 11):
        for t in range(4):
            sf[z, t, pl.ds(8, 32), :] = jnp.zeros((32, LANES), f32)

    shallow = DEPTH - 1
    near_k = z_messages(fine_view(kf), 4, shallow, 1) + z_messages(fine_view(cf), 4, 1, 1)
    side_k = x_messages(kf, 6, 4, 16)
    far_k = z_messages(fine_view(kf), 4, shallow, 2)
    last_k = x_messages(kf, 1, 1, 16) + x_messages(kf, 14, 1, 16)
    low_zk, mid_zk = [], []
    for hop in range(1, 7):
        low_zk += z_messages(low_view(3), 1, shallow, hop) + z_messages(low_view(4), 1, 1, hop)
    for hop in range(1, 4):
        mid_zk += z_messages(mid_view(km), 2, shallow, hop) + z_messages(mid_view(im), 2, 1, hop)
    low_xk = low_x_messages(3, shallow) + low_x_messages(4, 1)
    mid_xk = x_messages(km, 1, 12, 8) + x_messages(im, 5, 4, 8)
    relay_k = x_messages(kf, 2, 4, 16) + x_messages(kf, 10, 4, 16) + x_messages(cf, 5, 6, 16)

    def cycle_body(cycle, carry):
        opening = pl.when(cycle == 0)
        g = gf.at[cycle]
        near = z_messages(fine_view(g), 4, DEPTH, 1, cycle)
        far = z_messages(fine_view(g), 4, DEPTH, 2, cycle)
        side = x_messages(g, 6, 4, 16, cycle)
        relay = x_messages(g, 2, 4, 16, cycle) + x_messages(g, 10, 4, 16, cycle)
        last = x_messages(g, 0, 2, 16, cycle) + x_messages(g, 14, 2, 16, cycle)
        low_z, mid_z = [], []
        for hop in range(1, 7):
            low_z += z_messages(low_view(cycle), 1, DEPTH, hop, cycle)
        for hop in range(1, 4):
            mid_z += z_messages(mid_view(gm.at[cycle]), 2, DEPTH, hop, cycle)
        low_x = low_x_messages(cycle, DEPTH, cycle)
        mid_x = x_messages(gm.at[cycle], 0, 14, 8, cycle)

        @opening
        def _():
            cs, qs = restrict(tmp_c, 4, 4, 8), restrict(tmp_q, 4, 4, 8)
            for z in range(2):
                for t in range(2):
                    c, q = cs[z][t], qs[z][t]
                    diag = c * c + q
                    mid_c[z, t] = c
                    mid_q[z, t] = q
                    jm[z, t] = c / diag
                    km[6 + z, t, pl.ds(16, 8), :] = c * c / diag * (1.0 / 26.0)
                    im[6 + z, t, pl.ds(16, 8), :] = 1.0 / c
            c, q = restrict(mid_c, 2, 2, 4)[0][0], restrict(mid_q, 2, 2, 4)[0][0]
            diag = c * c + q
            jl[...] = c / diag
            lb[3, 6, 2] = c * c / diag * (1.0 / 26.0)
            lb[4, 6, 2] = 1.0 / c

        rs = restrict(tmp_r, 4, 4, 8)
        for z in range(2):
            for t in range(2):
                r = 4.0 * rs[z][t]
                mid_r[z, t] = r
                gm[cycle, 6 + z, t, pl.ds(16, 8), :] = r * jm[z, t]
        lb[cycle, 6, 2] = 4.0 * restrict(mid_r, 2, 2, 4)[0][0] * jl[...]

        start(low_z)

        @opening
        def _():
            start(low_zk)

        start(mid_z)

        @opening
        def _():
            start(mid_zk)

        start(near)

        @opening
        def _():
            start(near_k)

        start(side)

        @opening
        def _():
            start(side_k)

        start(far)

        @opening
        def _():
            start(far_k)

        arrived(low_z)
        start(low_x)

        @opening
        def _():
            arrived(low_zk)
            start(low_xk)

        arrived(mid_z)
        start(mid_x)

        @opening
        def _():
            arrived(mid_zk)
            start(mid_xk)

        arrived(near)
        start(relay)

        @opening
        def _():
            arrived(near_k)
            start(relay_k)

        arrived(far)
        start(last)

        @opening
        def _():
            arrived(far_k)
            start(last_k)

        arrived(low_x)

        @opening
        def _():
            arrived(low_xk)
            for kind, dst in ((3, kl), (4, il)):
                for block in range(5):
                    dst[:, 0, pl.ds(6 + 4 * block, 4), :] = lb[kind, :, block]

        for block in range(5):
            gl[:, 0, pl.ds(6 + 4 * block, 4), :] = lb[cycle, :, block]
        smooth(2, gl, kl, wl, dl, 1, 1, [(8, 16)])
        cut = pl.ds(12, 8)
        coarse = jnp.concatenate([wl[4, z, 0, cut, :] * il[z, 0, cut, :] for z in range(5, 8)], axis=0)
        wide = dot(coarse, spread)
        for z in range(3):
            for t in range(2):
                for dx in (0, 1):
                    pm[z, t, pl.ds(dx, 8, stride=2), :] = wide[8 * z:8 * z + 8, t * LANES:(t + 1) * LANES]

        arrived(mid_x)
        opening(lambda: arrived(mid_xk))
        smooth(1, gm.at[cycle], km, wm, dm, 2, 2, [(8, 24)])
        cut = pl.ds(12, 16)
        coarse = jnp.concatenate([
            wm[4, z, t, cut, :] * im[z, t, cut, :] + pm[(z - 6) // 2 + 1, t]
            for z in range(5, 9) for t in range(2)
        ], axis=0)
        wide = dot(coarse, spread)
        for z in range(4):
            for t in range(4):
                row, half = 16 * (2 * z + t // 2), t % 2
                for dx in (0, 1):
                    pf[z, t, pl.ds(dx, 16, stride=2), :] = wide[row:row + 16, half * LANES:(half + 1) * LANES]

        arrived(side + relay)
        opening(lambda: arrived(side_k + relay_k))
        chunks = [(8, 16), (24, 16)]
        smooth(0, g, kf, wf, df, 4, 4, chunks, lambda j: [(2 + j, 14 - j)])

        arrived(last)
        opening(lambda: arrived(last_k))
        smooth(0, g, kf, wf, df, 4, 4, chunks, lambda j: [(j, 2 + j), (14 - j, 16 - j)])

        for z in range(5, 11):
            for t in range(4):
                cut = pl.ds(8, 32)
                step = 0.5 * (wf[4, z, t, cut, :] + cf[z, t, cut, :] * pf[(z - 6) // 2 + 1, t])
                sf[z, t, cut, :] += step

        def residual(z, box):
            cut = pl.ds(16, 16)
            for t in range(4):
                here = sf[z, t, cut, :]
                scaled = gf[0, z, t, cut, :] - here + kf[z, t, cut, :] * (box[t] - here)
                plain = scaled * jf[z - 6, t]
                gf[cycle + 1, z, t, cut, :] = scaled
                tmp_r[z - 6, t] = plain
                out = pl.ds(t * LANES, LANES)
                sol_out[z - 6, :, out] = here / cf[z, t, cut, :]
                res_out[z - 6, :, out] = plain

        sweep(sf, 6, 10, 4, 16, 16, residual)
        sent(every)
        return carry

    lax.fori_loop(0, CYCLES, cycle_body, 0)
    assert len(once) <= ONCE and len(every) <= EVERY
    sent(once)


ONCE, EVERY = 80, 48


def shards(right_side, scale_field, mass_field, degrees, lower_bound, upper_bound):
    vmem = lambda *dims: pltpu.VMEM(dims, f32)
    fine, mid, low = (16, 4, 48, LANES), (14, 2, 40, LANES), (13, 1, 40, LANES)
    block = jax.ShapeDtypeStruct(right_side.shape, f32)
    whole = pl.BlockSpec(memory_space=pltpu.VMEM)
    scalar = pl.BlockSpec(memory_space=pltpu.SMEM)
    return pl.pallas_call(
        kernel,
        out_shape=(block, block),
        in_specs=[pl.BlockSpec(memory_space=pl.ANY)] * 3 + [scalar] * 3,
        out_specs=(whole, whole),
        scratch_shapes=[
            vmem(4, 16, 512), vmem(4, 16, 512), vmem(4, 16, 512),
            vmem(4, *fine), vmem(*fine), vmem(*fine), vmem(5, *fine), vmem(5, *fine), vmem(*fine),
            vmem(4, 4, 32, LANES), vmem(4, 4, 16, LANES), vmem(4, 4, 16, LANES), vmem(4, 4, 16, LANES), vmem(4, 4, 16, LANES),
            vmem(3, *mid), vmem(*mid), vmem(*mid), vmem(5, *mid), vmem(5, *mid),
            vmem(3, 2, 16, LANES), vmem(2, 2, 8, LANES), vmem(2, 2, 8, LANES), vmem(2, 2, 8, LANES), vmem(2, 2, 8, LANES),
            vmem(5, 13, 5, 4, LANES), vmem(*low), vmem(*low), vmem(*low), vmem(5, *low), vmem(5, *low),
            vmem(4, LANES),
            vmem(3, MAXDEG, 2, 8, LANES),
            pltpu.SemaphoreType.DMA((3,)),
            pltpu.SemaphoreType.DMA((ONCE,)), pltpu.SemaphoreType.DMA((ONCE,)),
            pltpu.SemaphoreType.DMA((CYCLES, EVERY)), pltpu.SemaphoreType.DMA((CYCLES, EVERY)),
        ],
        compiler_params=pltpu.CompilerParams(
            collective_id=0, has_side_effects=True, vmem_limit_bytes=56 * 1024 * 1024
        ),
    )(right_side, scale_field, mass_field, degrees, lower_bound, upper_bound)


def solution(mesh):
    cut = P("slab", "level", None)
    return jax.shard_map(
        shards, mesh=mesh, in_specs=(cut, cut, cut, P(), P(), P()), out_specs=(cut, cut), check_vma=False
    )
```

```python
import jax
import jax.numpy as jnp
from jax import lax
from jax.experimental import pallas as pl
from jax.experimental.pallas import tpu as pltpu
from jax.sharding import PartitionSpec as P

CYCLES = 3
MAXDEG = 6
DEPTH = 6
PEERS = 16
LANES = 128
MESH = pl.DeviceIdType.MESH
f32 = jnp.float32
bf16 = jnp.bfloat16


def split_matrices():
    row = lax.broadcasted_iota(jnp.int32, (LANES, LANES), 0)
    col = lax.broadcasted_iota(jnp.int32, (LANES, LANES), 1)
    spread = [jnp.where(row == half * 64 + col // 2, 1.0, 0.0) for half in (0, 1)]
    gather = [jnp.where(col == half * 64 + row // 2, 1.0, 0.0) for half in (0, 1)]
    quarter = [jnp.where(col == part * 32 + row // 4, 1.0, 0.0) for part in range(4)]
    return jnp.concatenate(quarter, axis=0).astype(bf16), jnp.concatenate(spread, axis=1).astype(bf16), jnp.concatenate(gather, axis=0).astype(bf16)


def dot(a, chosen):
    total = None
    for part in range(3):
        piece = a.astype(bf16)
        a = a - piece.astype(f32)
        product = jnp.dot(piece, chosen, preferred_element_type=f32)
        total = product if total is None else total + product
    return total


def kernel(
    rhs_in, scale_in, mass_in, degrees, lower, upper, sol_out, res_out,
    rhs, scale, mass,
    gf, kf, cf, wf, df, sf, pf, jf, tmp_c, tmp_q, tmp_r,
    gm, km, im, wm, dm, pm, jm, mid_c, mid_q,
    lb, gl, kl, il, wl, dl, jl,
    coef, load_sem, send_sem, recv_sem, cycle_send, cycle_recv,
):
    s = lax.axis_index("slab")
    l = lax.axis_index("level")
    once, every = [], []
    loads = [
        pltpu.make_async_copy(src, dst, load_sem.at[i])
        for i, (src, dst) in enumerate(((scale_in, scale), (mass_in, mass), (rhs_in, rhs)))
    ]

    def clear(refs, first, planes, rows):
        for ref in refs:
            for z in range(first, first + planes):
                for t in range(ref.shape[1]):
                    ref[z, t, pl.ds(*rows), :] = jnp.zeros((rows[1], LANES), f32)

    fine_refs = [gf.at[0], gf.at[1], gf.at[2], kf, cf]
    mid_refs = [gm.at[0], gm.at[1], gm.at[2], km, im]
    low_refs = [lb.at[kind] for kind in range(5)]

    @pl.when(s < 6)
    def _():
        clear(fine_refs, 0, 6, (8, 32))
        clear(mid_refs, 0, 6, (8, 24))
        clear(low_refs, 0, 6, (0, 4))

    @pl.when(s > 9)
    def _():
        clear(fine_refs, 10, 6, (8, 32))
        clear(mid_refs, 8, 6, (8, 24))
        clear(low_refs, 7, 6, (0, 4))

    @pl.when(l < 2)
    def _():
        clear(fine_refs, 0, 16, (8, 8))
        clear(mid_refs, 0, 14, (8, 8))
        clear([ref.at[:, pl.ds(0, 2)] for ref in low_refs], 0, 13, (0, 4))

    @pl.when(l > 13)
    def _():
        clear(fine_refs, 0, 16, (32, 8))
        clear(mid_refs, 0, 14, (24, 8))
        clear([ref.at[:, pl.ds(3, 2)] for ref in low_refs], 0, 13, (0, 4))

    barrier = pltpu.get_barrier_semaphore()
    for step in range(6, 0, -1):
        for sign in (1, -1):
            @pl.when((s + sign * step >= 0) & (s + sign * step < PEERS))
            def _(step=step, sign=sign):
                pl.semaphore_signal(barrier, inc=1, device_id={"slab": s + sign * step, "level": l}, device_id_type=MESH)
    for step in range(1, 3):
        for sign in (1, -1):
            @pl.when((l + sign * step >= 0) & (l + sign * step < PEERS))
            def _(step=step, sign=sign):
                pl.semaphore_signal(barrier, inc=1, device_id={"slab": s, "level": l + sign * step}, device_id_type=MESH)

    for load in loads:
        load.start()

    class Message:
        def __init__(self, src, dst, ds=0, dl=0, cycle=None):
            kept = once if cycle is None else every
            self.at = len(kept)
            kept.append(self)
            self.src, self.dst, self.ds, self.dl, self.cycle = src, dst, ds, dl, cycle

        def copy(self):
            if self.cycle is None:
                send, recv = send_sem.at[self.at], recv_sem.at[self.at]
            else:
                send, recv = cycle_send.at[self.cycle].at[self.at], cycle_recv.at[self.cycle].at[self.at]
            return pltpu.make_async_remote_copy(
                src_ref=self.src, dst_ref=self.dst, send_sem=send, recv_sem=recv,
                device_id={"slab": s + self.ds, "level": l + self.dl}, device_id_type=MESH,
            )

    def by_partner(messages, sign, act):
        groups = {}
        for m in messages:
            groups.setdefault((sign * m.ds, sign * m.dl), []).append(m)
        for (ds, dl), group in groups.items():
            at, step = (s, ds) if ds else (l, dl)

            @pl.when(at < PEERS - step if step > 0 else at >= -step)
            def _(group=group):
                for m in group:
                    act(m)

    def start(messages):
        by_partner(messages, 1, lambda m: m.copy().start())

    def arrived(messages):
        by_partner(messages, -1, lambda m: m.copy().wait_recv())

    def sent(messages):
        by_partner(messages, 1, lambda m: m.copy().wait_send())

    def z_messages(view, own, depth, hop, cycle=None):
        layers = max(0, min(own, depth - own * (hop - 1)))
        if layers == 0:
            return []
        gap = own * (hop - 1)
        top, bottom = 6 + own, 6
        return [
            Message(view(top - layers, layers), view(6 - gap - layers, layers), ds=hop, cycle=cycle),
            Message(view(bottom, layers), view(top + gap, layers), ds=-hop, cycle=cycle),
        ]

    def x_messages(buf, first, planes, width, cycle=None):
        cut = lambda row: buf.at[pl.ds(first, planes), :, pl.ds(row, 6), :]
        return [
            Message(cut(16 + width - 6), cut(10), dl=1, cycle=cycle),
            Message(cut(16), cut(16 + width), dl=-1, cycle=cycle),
        ]

    def low_x_messages(kind, depth, cycle=None):
        cut = lambda block: lb.at[kind].at[pl.ds(6 - depth, 1 + 2 * depth), block]
        return [Message(cut(2), cut(2 - step), dl=step, cycle=cycle) for step in (1, -1, 2, -2)]

    fine_view = lambda buf: (lambda first, layers: buf.at[pl.ds(first, layers), :, pl.ds(16, 16), :])
    mid_view = lambda buf: (lambda first, layers: buf.at[pl.ds(first, layers), :, pl.ds(16, 8), :])
    low_view = lambda kind: (lambda first, layers: lb.at[kind].at[pl.ds(first, layers), 2])

    for grid in range(3):
        low_b = jnp.full((8, LANES), lower[grid], f32)
        high_b = jnp.full((8, LANES), upper[grid], f32)
        degree = jnp.full((8, LANES), degrees[grid], jnp.int32)
        centre = (high_b + low_b) * 0.5
        radius = (high_b - low_b) * 0.5
        ratio = centre / radius
        rho = 1.0 / ratio
        coef[grid, 0, 0] = 1.0 / centre
        for j in range(1, MAXDEG):
            rho_new = 1.0 / (2.0 * ratio - rho)
            active = j < degree
            coef[grid, j, 0] = jnp.where(active, rho_new * rho, 0.0)
            coef[grid, j, 1] = jnp.where(active, 2.0 * rho_new / radius, 0.0)
            rho = rho_new

    quarter, spread, gather = split_matrices()
    lane = lax.broadcasted_iota(jnp.int32, (1, LANES), 1)

    def tile_rows(v, rows):
        return jnp.concatenate([v] * (rows // 8), axis=0) if rows > 8 else v

    def x_sum(ref, z, tiles, r0, rows):
        return tuple(
            ref[z, t, pl.ds(r0 - 1, rows), :] + ref[z, t, pl.ds(r0, rows), :] + ref[z, t, pl.ds(r0 + 1, rows), :]
            for t in range(tiles)
        )

    def y_sum(vals):
        right = [pltpu.roll(v, 1, 1) for v in vals]
        left = [pltpu.roll(v, LANES - 1, 1) for v in vals]
        out = []
        for t, v in enumerate(vals):
            before = right[t - 1] if t > 0 else 0.0
            after = left[t + 1] if t + 1 < len(vals) else 0.0
            out.append(v + jnp.where(lane == 0, before, right[t]) + jnp.where(lane == LANES - 1, after, left[t]))
        return out

    def sweep(src, lo, hi, tiles, r0, rows, use):
        first = (x_sum(src, lo - 1, tiles, r0, rows), x_sum(src, lo, tiles, r0, rows))

        def plane(z, carry):
            below, here = carry
            above = x_sum(src, z + 1, tiles, r0, rows)
            box = y_sum([a + b + c for a, b, c in zip(below, here, above)])
            use(z, box)
            return here, above

        for z in range(lo, hi):
            first = plane(z, first)

    def smooth(grid, g, k, w, d, own, tiles, chunks, spans=None):
        planes = own + 2 * DEPTH
        for j in range(1, MAXDEG):
            new, turn = w.at[j - 1], d.at[j - 1]
            old, past = (g, None) if j == 1 else (w.at[j - 2], d.at[j - 2])
            parts = [(j, planes - j)] if spans is None else spans(j)
            for (r0, rows), (lo, hi) in [(chunk, part) for chunk in chunks for part in parts]:
                a = tile_rows(coef[grid, j, 0], rows)
                b = tile_rows(coef[grid, j, 1], rows)
                first = tile_rows(coef[grid, 0, 0], rows)

                def use(z, box, j=j, r0=r0, rows=rows, a=a, b=b, first=first, new=new, old=old, turn=turn, past=past):
                    cut = pl.ds(r0, rows)
                    for t in range(tiles):
                        source = g[z, t, cut, :]
                        if j == 1:
                            here = source * first
                            total = box[t] * first
                            direction = here
                        else:
                            here = old[z, t, cut, :]
                            total = box[t]
                            direction = past[z, t, cut, :]
                        defect = (source - here) + k[z, t, cut, :] * (total - here)
                        direction = a * direction + b * defect
                        turn[z, t, cut, :] = direction
                        new[z, t, cut, :] = here + direction

                sweep(old, lo, hi, tiles, r0, rows, use)

    def restrict(src, planes, tiles, rows):
        sums = []
        for z in range(planes // 2):
            for t in range(tiles):
                total = None
                for dz in (0, 1):
                    for dx in (0, 1):
                        part = src[2 * z + dz, t, pl.ds(dx, rows, stride=2), :]
                        total = part if total is None else total + part
                sums.append(total * 0.125)
        pairs = [jnp.concatenate(sums[at:at + 2], axis=1) for at in range(0, len(sums), 2)]
        joined = dot(jnp.concatenate(pairs, axis=0), gather)
        half = tiles // 2
        return [
            [joined[rows * (z * half + o):rows * (z * half + o + 1)] for o in range(half)] for z in range(planes // 2)
        ]

    for load in loads:
        load.wait()
    for z in range(4):
        for t in range(4):
            cut = pl.ds(t * LANES, LANES)
            c = scale[z, :, cut]
            q = mass[z, :, cut]
            diag = c * c + q
            inverse = 1.0 / diag
            tmp_c[z, t, pl.ds(0, 16), :] = c
            tmp_q[z, t, pl.ds(0, 16), :] = q
            jf[z, t] = diag / c
            b = rhs[z, :, cut]
            tmp_r[z, t, pl.ds(0, 16), :] = b
            kf[6 + z, t, pl.ds(16, 16), :] = c * c * inverse * (1.0 / 26.0)
            cf[6 + z, t, pl.ds(16, 16), :] = c
            gf[0, 6 + z, t, pl.ds(16, 16), :] = c * inverse * b

    up, down = jnp.minimum(s, 6), jnp.minimum(PEERS - 1 - s, 6)
    left, right = jnp.minimum(l, 2), jnp.minimum(PEERS - 1 - l, 2)
    pl.semaphore_wait(barrier, up + down + left + right)

    for z in range(5, 11):
        for t in range(4):
            sf[z, t, pl.ds(8, 32), :] = jnp.zeros((32, LANES), f32)

    shallow = DEPTH - 1
    near_k = z_messages(fine_view(kf), 4, shallow, 1) + z_messages(fine_view(cf), 4, 1, 1)
    side_k = x_messages(kf, 6, 4, 16)
    far_k = z_messages(fine_view(kf), 4, shallow, 2)
    last_k = x_messages(kf, 1, 1, 16) + x_messages(kf, 14, 1, 16)
    low_zk, mid_zk = [], []
    for hop in range(1, 7):
        low_zk += z_messages(low_view(3), 1, shallow, hop) + z_messages(low_view(4), 1, 1, hop)
    for hop in range(1, 4):
        mid_zk += z_messages(mid_view(km), 2, shallow, hop) + z_messages(mid_view(im), 2, 1, hop)
    low_xk = low_x_messages(3, shallow) + low_x_messages(4, 1)
    mid_xk = x_messages(km, 1, 12, 8) + x_messages(im, 5, 4, 8)
    relay_k = x_messages(kf, 2, 4, 16) + x_messages(kf, 10, 4, 16) + x_messages(cf, 5, 6, 16)

    def cycle_body(cycle, carry):
        opening = pl.when(cycle == 0)
        g = gf.at[cycle]
        near = z_messages(fine_view(g), 4, DEPTH, 1, cycle)
        far = z_messages(fine_view(g), 4, DEPTH, 2, cycle)
        side = x_messages(g, 6, 4, 16, cycle)
        relay = x_messages(g, 2, 4, 16, cycle) + x_messages(g, 10, 4, 16, cycle)
        last = x_messages(g, 0, 2, 16, cycle) + x_messages(g, 14, 2, 16, cycle)
        low_z, mid_z = [], []
        for hop in range(6, 0, -1):
            low_z += z_messages(low_view(cycle), 1, DEPTH, hop, cycle)
        for hop in range(3, 0, -1):
            mid_z += z_messages(mid_view(gm.at[cycle]), 2, DEPTH, hop, cycle)
        low_x = low_x_messages(cycle, DEPTH, cycle)
        mid_x = x_messages(gm.at[cycle], 0, 14, 8, cycle)

        @opening
        def _():
            cs, qs = restrict(tmp_c, 4, 4, 8), restrict(tmp_q, 4, 4, 8)
            for z in range(2):
                for t in range(2):
                    c, q = cs[z][t], qs[z][t]
                    diag = c * c + q
                    mid_c[z, t, pl.ds(0, 8), :] = c
                    mid_q[z, t, pl.ds(0, 8), :] = q
                    jm[z, t] = c / diag
                    km[6 + z, t, pl.ds(16, 8), :] = c * c / diag * (1.0 / 26.0)
                    im[6 + z, t, pl.ds(16, 8), :] = 1.0 / c
            c, q = restrict(mid_c, 2, 2, 4)[0][0], restrict(mid_q, 2, 2, 4)[0][0]
            diag = c * c + q
            jl[pl.ds(0, 4), :] = c / diag
            lb[3, 6, 2] = c * c / diag * (1.0 / 26.0)
            lb[4, 6, 2] = 1.0 / c

        sums = []
        for t in range(4):
            total = None
            for z in range(4):
                for dx in range(4):
                    part = tmp_r[z, t, pl.ds(dx, 4, stride=4), :]
                    total = part if total is None else total + part
            sums.append(total * 0.25)
        lb[cycle, 6, 2] = dot(jnp.concatenate(sums, axis=1), quarter) * jl[pl.ds(0, 4), :]
        rs = restrict(tmp_r, 4, 4, 8)
        for z in range(2):
            for t in range(2):
                r = 4.0 * rs[z][t]
                gm[cycle, 6 + z, t, pl.ds(16, 8), :] = r * jm[z, t]

        start(low_z)

        @opening
        def _():
            start(low_zk)

        start(mid_z)

        @opening
        def _():
            start(mid_zk)

        start(near)

        @opening
        def _():
            start(near_k)

        start(side)

        @opening
        def _():
            start(side_k)

        start(far)

        @opening
        def _():
            start(far_k)

        arrived(low_z)
        start(low_x)

        @opening
        def _():
            arrived(low_zk)
            start(low_xk)

        arrived(mid_z)
        start(mid_x)

        @opening
        def _():
            arrived(mid_zk)
            start(mid_xk)

        arrived(near)
        start(relay)

        @opening
        def _():
            arrived(near_k)
            start(relay_k)

        arrived(far)
        start(last)

        @opening
        def _():
            arrived(far_k)
            start(last_k)

        arrived(low_x)

        @opening
        def _():
            arrived(low_xk)
            for kind, dst in ((3, kl), (4, il)):
                for block in range(5):
                    dst[:, 0, pl.ds(6 + 4 * block, 4), :] = lb[kind, :, block]

        for block in range(5):
            gl[:, 0, pl.ds(6 + 4 * block, 4), :] = lb[cycle, :, block]
        smooth(2, gl, kl, wl, dl, 1, 1, [(8, 16)])
        cut = pl.ds(12, 8)
        coarse = jnp.concatenate([wl[4, z, 0, cut, :] * il[z, 0, cut, :] for z in range(5, 8)], axis=0)
        wide = dot(coarse, spread)
        for z in range(3):
            for t in range(2):
                for dx in (0, 1):
                    pm[z, t, pl.ds(dx, 8, stride=2), :] = wide[8 * z:8 * z + 8, t * LANES:(t + 1) * LANES]

        arrived(mid_x)
        opening(lambda: arrived(mid_xk))
        smooth(1, gm.at[cycle], km, wm, dm, 2, 2, [(8, 24)])
        cut = pl.ds(12, 16)
        coarse = jnp.concatenate([
            wm[4, z, t, cut, :] * im[z, t, cut, :] + pm[(z - 6) // 2 + 1, t, pl.ds(0, 16), :]
            for z in range(5, 9) for t in range(2)
        ], axis=0)
        wide = dot(coarse, spread)
        for z in range(4):
            for t in range(4):
                row, half = 16 * (2 * z + t // 2), t % 2
                for dx in (0, 1):
                    pf[z, t, pl.ds(dx, 16, stride=2), :] = wide[row:row + 16, half * LANES:(half + 1) * LANES]

        opening(lambda: arrived(relay_k))
        for z in range(5, 11):
            for t in range(4):
                cut = pl.ds(8, 32)
                sf[z, t, cut, :] += 0.5 * (cf[z, t, cut, :] * pf[(z - 6) // 2 + 1, t, pl.ds(0, 32), :])

        arrived(side + relay)
        opening(lambda: arrived(side_k))
        chunks = [(8, 16), (24, 16)]
        smooth(0, g, kf, wf, df, 4, 4, chunks, lambda j: [(2 + j, 14 - j)])

        arrived(last)
        opening(lambda: arrived(last_k))
        smooth(0, g, kf, wf, df, 4, 4, chunks, lambda j: [(j, 2 + j), (14 - j, 16 - j)])

        for z in range(5, 11):
            for t in range(4):
                cut = pl.ds(8, 32)
                sf[z, t, cut, :] += 0.5 * wf[4, z, t, cut, :]

        def residual(z, box):
            cut = pl.ds(16, 16)
            for t in range(4):
                here = sf[z, t, cut, :]
                scaled = gf[0, z, t, cut, :] - here + kf[z, t, cut, :] * (box[t] - here)
                plain = scaled * jf[z - 6, t]
                gf[cycle + 1, z, t, cut, :] = scaled
                tmp_r[z - 6, t, pl.ds(0, 16), :] = plain
                out = pl.ds(t * LANES, LANES)
                sol_out[z - 6, :, out] = here
                res_out[z - 6, :, out] = scaled

        sweep(sf, 6, 10, 4, 16, 16, residual)
        sent(every)
        return carry

    lax.fori_loop(0, CYCLES, cycle_body, 0)
    assert len(once) <= ONCE and len(every) <= EVERY
    sent(once)


ONCE, EVERY = 80, 48


def shards(right_side, scale_field, mass_field, degrees, lower_bound, upper_bound):
    vmem = lambda *dims: pltpu.VMEM(dims, f32)
    fine, mid, low = (16, 4, 48, LANES), (14, 2, 40, LANES), (13, 1, 40, LANES)
    block = jax.ShapeDtypeStruct(right_side.shape, f32)
    whole = pl.BlockSpec(memory_space=pltpu.VMEM)
    scalar = pl.BlockSpec(memory_space=pltpu.SMEM)
    weighted, scaled = pl.pallas_call(
        kernel,
        out_shape=(block, block),
        in_specs=[pl.BlockSpec(memory_space=pl.ANY)] * 3 + [scalar] * 3,
        out_specs=(whole, whole),
        scratch_shapes=[
            vmem(4, 16, 512), vmem(4, 16, 512), vmem(4, 16, 512),
            vmem(4, *fine), vmem(*fine), vmem(*fine), vmem(5, *fine), vmem(5, *fine), vmem(*fine),
            vmem(4, 4, 40, LANES), vmem(4, 4, 16, LANES), vmem(4, 4, 24, LANES), vmem(4, 4, 24, LANES), vmem(4, 4, 24, LANES),
            vmem(3, *mid), vmem(*mid), vmem(*mid), vmem(5, *mid), vmem(5, *mid),
            vmem(3, 2, 24, LANES), vmem(2, 2, 8, LANES), vmem(2, 2, 16, LANES), vmem(2, 2, 16, LANES),
            vmem(6, 13, 5, 4, LANES), vmem(*low), vmem(*low), vmem(*low), vmem(5, *low), vmem(5, *low),
            vmem(8, LANES),
            vmem(3, MAXDEG, 2, 8, LANES),
            pltpu.SemaphoreType.DMA((3,)),
            pltpu.SemaphoreType.DMA((ONCE,)), pltpu.SemaphoreType.DMA((ONCE,)),
            pltpu.SemaphoreType.DMA((CYCLES, EVERY)), pltpu.SemaphoreType.DMA((CYCLES, EVERY)),
        ],
        compiler_params=pltpu.CompilerParams(
            collective_id=0, has_side_effects=True, vmem_limit_bytes=56 * 1024 * 1024
        ),
    )(right_side, scale_field, mass_field, degrees, lower_bound, upper_bound)
    inverse = 1.0 / scale_field
    return weighted * inverse, scaled * (scale_field + mass_field * inverse)


def solution(mesh):
    cut = P("slab", "level", None)
    return jax.shard_map(
        shards, mesh=mesh, in_specs=(cut, cut, cut, P(), P(), P()), out_specs=(cut, cut), check_vma=False
    )
```

```python
import jax
import jax.numpy as jnp
from jax import lax
from jax.experimental import pallas as pl
from jax.experimental.pallas import tpu as pltpu
from jax.sharding import PartitionSpec as P

CYCLES = 3
MAXDEG = 6
DEPTH = 6
PEERS = 16
LANES = 128
MESH = pl.DeviceIdType.MESH
f32 = jnp.float32
bf16 = jnp.bfloat16


def split_matrices():
    row = lax.broadcasted_iota(jnp.int32, (LANES, LANES), 0)
    col = lax.broadcasted_iota(jnp.int32, (LANES, LANES), 1)
    spread = [jnp.where(row == half * 64 + col // 2, 1.0, 0.0) for half in (0, 1)]
    gather = [jnp.where(col == half * 64 + row // 2, 1.0, 0.0) for half in (0, 1)]
    quarter = [jnp.where(col == part * 32 + row // 4, 1.0, 0.0) for part in range(4)]
    return jnp.concatenate(quarter, axis=0).astype(bf16), jnp.concatenate(spread, axis=1).astype(bf16), jnp.concatenate(gather, axis=0).astype(bf16)


def dot(a, chosen):
    total = None
    for part in range(3):
        piece = a.astype(bf16)
        a = a - piece.astype(f32)
        product = jnp.dot(piece, chosen, preferred_element_type=f32)
        total = product if total is None else total + product
    return total


def kernel(
    rhs_in, scale_in, mass_in, degrees, lower, upper, sol_out, res_out,
    rhs, scale, mass,
    gf, kf, cf, wf, df, sf, pf, jf, tmp_c, tmp_q, tmp_r,
    gm, km, im, wm, dm, pm, jm,
    lb, gl, kl, il, wl, dl, jl,
    coef, load_sem, send_sem, recv_sem, cycle_send, cycle_recv,
):
    s = lax.axis_index("slab")
    l = lax.axis_index("level")
    once, every = [], []
    loads = [
        pltpu.make_async_copy(src, dst, load_sem.at[i])
        for i, (src, dst) in enumerate(((scale_in, scale), (mass_in, mass), (rhs_in, rhs)))
    ]

    def clear(refs, first, planes, rows):
        for ref in refs:
            for z in range(first, first + planes):
                for t in range(ref.shape[1]):
                    ref[z, t, pl.ds(*rows), :] = jnp.zeros((rows[1], LANES), f32)

    fine_refs = [gf.at[0], gf.at[1], gf.at[2], kf, cf]
    mid_refs = [gm.at[0], gm.at[1], gm.at[2], km, im]
    low_refs = [lb.at[kind] for kind in range(5)]

    @pl.when(s < 6)
    def _():
        clear(fine_refs, 0, 6, (8, 32))
        clear(mid_refs, 0, 6, (8, 24))
        clear(low_refs, 0, 6, (0, 4))

    @pl.when(s > 9)
    def _():
        clear(fine_refs, 10, 6, (8, 32))
        clear(mid_refs, 8, 6, (8, 24))
        clear(low_refs, 7, 6, (0, 4))

    @pl.when(l < 2)
    def _():
        clear(fine_refs, 0, 16, (8, 8))
        clear(mid_refs, 0, 14, (8, 8))
        clear([ref.at[:, pl.ds(0, 2)] for ref in low_refs], 0, 13, (0, 4))

    @pl.when(l > 13)
    def _():
        clear(fine_refs, 0, 16, (32, 8))
        clear(mid_refs, 0, 14, (24, 8))
        clear([ref.at[:, pl.ds(3, 2)] for ref in low_refs], 0, 13, (0, 4))

    barrier = pltpu.get_barrier_semaphore()
    for step in range(6, 0, -1):
        for sign in (1, -1):
            @pl.when((s + sign * step >= 0) & (s + sign * step < PEERS))
            def _(step=step, sign=sign):
                pl.semaphore_signal(barrier, inc=1, device_id={"slab": s + sign * step, "level": l}, device_id_type=MESH)
    for step in range(1, 3):
        for sign in (1, -1):
            @pl.when((l + sign * step >= 0) & (l + sign * step < PEERS))
            def _(step=step, sign=sign):
                pl.semaphore_signal(barrier, inc=1, device_id={"slab": s, "level": l + sign * step}, device_id_type=MESH)

    for load in loads:
        load.start()

    class Message:
        def __init__(self, src, dst, ds=0, dl=0, cycle=None):
            kept = once if cycle is None else every
            self.at = len(kept)
            kept.append(self)
            self.src, self.dst, self.ds, self.dl, self.cycle = src, dst, ds, dl, cycle

        def copy(self):
            if self.cycle is None:
                send, recv = send_sem.at[self.at], recv_sem.at[self.at]
            else:
                send, recv = cycle_send.at[self.cycle].at[self.at], cycle_recv.at[self.cycle].at[self.at]
            return pltpu.make_async_remote_copy(
                src_ref=self.src, dst_ref=self.dst, send_sem=send, recv_sem=recv,
                device_id={"slab": s + self.ds, "level": l + self.dl}, device_id_type=MESH,
            )

    def by_partner(messages, sign, act):
        groups = {}
        for m in messages:
            groups.setdefault((sign * m.ds, sign * m.dl), []).append(m)
        for (ds, dl), group in groups.items():
            at, step = (s, ds) if ds else (l, dl)

            @pl.when(at < PEERS - step if step > 0 else at >= -step)
            def _(group=group):
                for m in group:
                    act(m)

    def start(messages):
        by_partner(messages, 1, lambda m: m.copy().start())

    def arrived(messages):
        by_partner(messages, -1, lambda m: m.copy().wait_recv())

    def sent(messages):
        by_partner(messages, 1, lambda m: m.copy().wait_send())

    def z_messages(view, own, depth, hop, cycle=None):
        layers = max(0, min(own, depth - own * (hop - 1)))
        if layers == 0:
            return []
        gap = own * (hop - 1)
        top, bottom = 6 + own, 6
        return [
            Message(view(top - layers, layers), view(6 - gap - layers, layers), ds=hop, cycle=cycle),
            Message(view(bottom, layers), view(top + gap, layers), ds=-hop, cycle=cycle),
        ]

    def x_messages(buf, first, planes, width, cycle=None):
        cut = lambda row: buf.at[pl.ds(first, planes), :, pl.ds(row, 6), :]
        return [
            Message(cut(16 + width - 6), cut(10), dl=1, cycle=cycle),
            Message(cut(16), cut(16 + width), dl=-1, cycle=cycle),
        ]

    def low_x_messages(kind, depth, cycle=None):
        cut = lambda block: lb.at[kind].at[pl.ds(6 - depth, 1 + 2 * depth), block]
        return [Message(cut(2), cut(2 - step), dl=step, cycle=cycle) for step in (1, -1, 2, -2)]

    fine_view = lambda buf: (lambda first, layers: buf.at[pl.ds(first, layers), :, pl.ds(16, 16), :])
    mid_view = lambda buf: (lambda first, layers: buf.at[pl.ds(first, layers), :, pl.ds(16, 8), :])
    low_view = lambda kind: (lambda first, layers: lb.at[kind].at[pl.ds(first, layers), 2])

    for grid in range(3):
        low_b = jnp.full((8, LANES), lower[grid], f32)
        high_b = jnp.full((8, LANES), upper[grid], f32)
        degree = jnp.full((8, LANES), degrees[grid], jnp.int32)
        centre = (high_b + low_b) * 0.5
        radius = (high_b - low_b) * 0.5
        ratio = centre / radius
        rho = 1.0 / ratio
        coef[grid, 0, 0] = 1.0 / centre
        for j in range(1, MAXDEG):
            rho_new = 1.0 / (2.0 * ratio - rho)
            active = j < degree
            coef[grid, j, 0] = jnp.where(active, rho_new * rho, 0.0)
            coef[grid, j, 1] = jnp.where(active, 2.0 * rho_new / radius, 0.0)
            rho = rho_new

    quarter, spread, gather = split_matrices()
    lane = lax.broadcasted_iota(jnp.int32, (1, LANES), 1)

    def tile_rows(v, rows):
        return jnp.concatenate([v] * (rows // 8), axis=0) if rows > 8 else v

    def x_sum(ref, z, tiles, r0, rows):
        return tuple(
            ref[z, t, pl.ds(r0 - 1, rows), :] + ref[z, t, pl.ds(r0, rows), :] + ref[z, t, pl.ds(r0 + 1, rows), :]
            for t in range(tiles)
        )

    def y_sum(vals):
        right = [pltpu.roll(v, 1, 1) for v in vals]
        left = [pltpu.roll(v, LANES - 1, 1) for v in vals]
        out = []
        for t, v in enumerate(vals):
            before = right[t - 1] if t > 0 else 0.0
            after = left[t + 1] if t + 1 < len(vals) else 0.0
            out.append(v + jnp.where(lane == 0, before, right[t]) + jnp.where(lane == LANES - 1, after, left[t]))
        return out

    def sweep(src, lo, hi, tiles, r0, rows, use):
        first = (x_sum(src, lo - 1, tiles, r0, rows), x_sum(src, lo, tiles, r0, rows))

        def plane(z, carry):
            below, here = carry
            above = x_sum(src, z + 1, tiles, r0, rows)
            box = y_sum([a + b + c for a, b, c in zip(below, here, above)])
            use(z, box)
            return here, above

        for z in range(lo, hi):
            first = plane(z, first)

    def smooth(grid, g, k, w, d, own, tiles, chunks, spans=None):
        planes = own + 2 * DEPTH
        for j in range(1, MAXDEG):
            new, turn = w.at[j - 1], d.at[j - 1]
            old, past = (g, None) if j == 1 else (w.at[j - 2], d.at[j - 2])
            parts = [(j, planes - j)] if spans is None else spans(j)
            for (r0, rows), (lo, hi) in [(chunk, part) for chunk in chunks for part in parts]:
                a = tile_rows(coef[grid, j, 0], rows)
                b = tile_rows(coef[grid, j, 1], rows)
                first = tile_rows(coef[grid, 0, 0], rows)

                def use(z, box, j=j, r0=r0, rows=rows, a=a, b=b, first=first, new=new, old=old, turn=turn, past=past):
                    cut = pl.ds(r0, rows)
                    for t in range(tiles):
                        source = g[z, t, cut, :]
                        if j == 1:
                            here = source * first
                            total = box[t] * first
                            direction = here
                        else:
                            here = old[z, t, cut, :]
                            total = box[t]
                            direction = past[z, t, cut, :]
                        defect = (source - here) + k[z, t, cut, :] * (total - here)
                        direction = a * direction + b * defect
                        turn[z, t, cut, :] = direction
                        new[z, t, cut, :] = here + direction

                sweep(old, lo, hi, tiles, r0, rows, use)

    def restrict(src, planes, tiles, rows):
        sums = []
        for z in range(planes // 2):
            for t in range(tiles):
                total = None
                for dz in (0, 1):
                    for dx in (0, 1):
                        part = src[2 * z + dz, t, pl.ds(dx, rows, stride=2), :]
                        total = part if total is None else total + part
                sums.append(total * 0.125)
        pairs = [jnp.concatenate(sums[at:at + 2], axis=1) for at in range(0, len(sums), 2)]
        joined = dot(jnp.concatenate(pairs, axis=0), gather)
        half = tiles // 2
        return [
            [joined[rows * (z * half + o):rows * (z * half + o + 1)] for o in range(half)] for z in range(planes // 2)
        ]

    def restrict_twice(src):
        sums = []
        for t in range(4):
            total = None
            for z in range(4):
                for dx in range(4):
                    part = src[z, t, pl.ds(dx, 4, stride=4), :]
                    total = part if total is None else total + part
            sums.append(total * (1.0 / 64.0))
        return dot(jnp.concatenate(sums, axis=1), quarter)

    for load in loads:
        load.wait()
    for z in range(4):
        for t in range(4):
            cut = pl.ds(t * LANES, LANES)
            c = scale[z, :, cut]
            q = mass[z, :, cut]
            diag = c * c + q
            inverse = 1.0 / diag
            tmp_c[z, t, pl.ds(0, 16), :] = c
            tmp_q[z, t, pl.ds(0, 16), :] = q
            jf[z, t] = diag / c
            b = rhs[z, :, cut]
            tmp_r[z, t, pl.ds(0, 16), :] = b
            kf[6 + z, t, pl.ds(16, 16), :] = c * c * inverse * (1.0 / 26.0)
            cf[6 + z, t, pl.ds(16, 16), :] = c
            gf[0, 6 + z, t, pl.ds(16, 16), :] = c * inverse * b

    up, down = jnp.minimum(s, 6), jnp.minimum(PEERS - 1 - s, 6)
    left, right = jnp.minimum(l, 2), jnp.minimum(PEERS - 1 - l, 2)
    pl.semaphore_wait(barrier, up + down + left + right)

    for z in range(5, 11):
        for t in range(4):
            sf[z, t, pl.ds(8, 32), :] = jnp.zeros((32, LANES), f32)

    shallow = DEPTH - 1
    near_k = z_messages(fine_view(kf), 4, shallow, 1) + z_messages(fine_view(cf), 4, 1, 1)
    side_k = x_messages(kf, 6, 4, 16)
    far_k = z_messages(fine_view(kf), 4, shallow, 2)
    last_k = x_messages(kf, 1, 1, 16) + x_messages(kf, 14, 1, 16)
    low_zk, mid_zk = [], []
    for hop in range(1, 7):
        low_zk += z_messages(low_view(3), 1, shallow, hop) + z_messages(low_view(4), 1, 1, hop)
    for hop in range(1, 4):
        mid_zk += z_messages(mid_view(km), 2, shallow, hop) + z_messages(mid_view(im), 2, 1, hop)
    low_xk = low_x_messages(3, shallow) + low_x_messages(4, 1)
    mid_xk = x_messages(km, 1, 12, 8) + x_messages(im, 5, 4, 8)
    relay_k = x_messages(kf, 2, 4, 16) + x_messages(kf, 10, 4, 16) + x_messages(cf, 5, 6, 16)

    def cycle_body(cycle, carry):
        opening = pl.when(cycle == 0)
        g = gf.at[cycle]
        near = z_messages(fine_view(g), 4, DEPTH, 1, cycle)
        far = z_messages(fine_view(g), 4, DEPTH, 2, cycle)
        side = x_messages(g, 6, 4, 16, cycle)
        relay = x_messages(g, 2, 4, 16, cycle) + x_messages(g, 10, 4, 16, cycle)
        last = x_messages(g, 0, 2, 16, cycle) + x_messages(g, 14, 2, 16, cycle)
        low_z, mid_z = [], []
        for hop in range(6, 0, -1):
            low_z += z_messages(low_view(cycle), 1, DEPTH, hop, cycle)
        for hop in range(3, 0, -1):
            mid_z += z_messages(mid_view(gm.at[cycle]), 2, DEPTH, hop, cycle)
        low_x = low_x_messages(cycle, DEPTH, cycle)
        mid_x = x_messages(gm.at[cycle], 0, 14, 8, cycle)

        @opening
        def _():
            cs, qs = restrict(tmp_c, 4, 4, 8), restrict(tmp_q, 4, 4, 8)
            for z in range(2):
                for t in range(2):
                    c, q = cs[z][t], qs[z][t]
                    diag = c * c + q
                    jm[z, t] = c / diag
                    km[6 + z, t, pl.ds(16, 8), :] = c * c / diag * (1.0 / 26.0)
                    im[6 + z, t, pl.ds(16, 8), :] = 1.0 / c
            c, q = restrict_twice(tmp_c), restrict_twice(tmp_q)
            diag = c * c + q
            jl[pl.ds(0, 4), :] = c / diag
            lb[3, 6, 2] = c * c / diag * (1.0 / 26.0)
            lb[4, 6, 2] = 1.0 / c

        lb[cycle, 6, 2] = 16.0 * restrict_twice(tmp_r) * jl[pl.ds(0, 4), :]
        rs = restrict(tmp_r, 4, 4, 8)
        for z in range(2):
            for t in range(2):
                r = 4.0 * rs[z][t]
                gm[cycle, 6 + z, t, pl.ds(16, 8), :] = r * jm[z, t]

        start(low_z)

        @opening
        def _():
            start(low_zk)

        start(mid_z)

        @opening
        def _():
            start(mid_zk)

        start(near)

        @opening
        def _():
            start(near_k)

        start(side)

        @opening
        def _():
            start(side_k)

        start(far)

        @opening
        def _():
            start(far_k)

        arrived(low_z)
        start(low_x)

        @opening
        def _():
            arrived(low_zk)
            start(low_xk)

        arrived(mid_z)
        start(mid_x)

        @opening
        def _():
            arrived(mid_zk)
            start(mid_xk)

        arrived(near)
        start(relay)

        @opening
        def _():
            arrived(near_k)
            start(relay_k)

        arrived(far)
        start(last)

        @opening
        def _():
            arrived(far_k)
            start(last_k)

        arrived(low_x)

        @opening
        def _():
            arrived(low_xk)
            for kind, dst in ((3, kl), (4, il)):
                for block in range(5):
                    dst[:, 0, pl.ds(6 + 4 * block, 4), :] = lb[kind, :, block]

        for block in range(5):
            gl[:, 0, pl.ds(6 + 4 * block, 4), :] = lb[cycle, :, block]
        smooth(2, gl, kl, wl, dl, 1, 1, [(8, 16)])
        cut = pl.ds(12, 8)
        coarse = jnp.concatenate([wl[4, z, 0, cut, :] * il[z, 0, cut, :] for z in range(5, 8)], axis=0)
        wide = dot(coarse, spread)
        for z in range(3):
            for t in range(2):
                for dx in (0, 1):
                    pm[z, t, pl.ds(dx, 8, stride=2), :] = wide[8 * z:8 * z + 8, t * LANES:(t + 1) * LANES]

        arrived(mid_x)
        opening(lambda: arrived(mid_xk))
        smooth(1, gm.at[cycle], km, wm, dm, 2, 2, [(8, 24)])
        cut = pl.ds(12, 16)
        coarse = jnp.concatenate([
            wm[4, z, t, cut, :] * im[z, t, cut, :] + pm[(z - 6) // 2 + 1, t, pl.ds(0, 16), :]
            for z in range(5, 9) for t in range(2)
        ], axis=0)
        wide = dot(coarse, spread)
        for z in range(4):
            for t in range(4):
                row, half = 16 * (2 * z + t // 2), t % 2
                for dx in (0, 1):
                    pf[z, t, pl.ds(dx, 16, stride=2), :] = wide[row:row + 16, half * LANES:(half + 1) * LANES]

        opening(lambda: arrived(relay_k))
        for z in range(5, 11):
            for t in range(4):
                cut = pl.ds(8, 32)
                sf[z, t, cut, :] += 0.5 * (cf[z, t, cut, :] * pf[(z - 6) // 2 + 1, t, pl.ds(0, 32), :])

        arrived(side + relay)
        opening(lambda: arrived(side_k))
        chunks = [(8, 16), (24, 16)]
        smooth(0, g, kf, wf, df, 4, 4, chunks, lambda j: [(2 + j, 14 - j)])

        sent(low_z + mid_z + near + side + far + relay + low_x + mid_x)
        opening(lambda: sent(once))
        arrived(last)
        opening(lambda: arrived(last_k))
        smooth(0, g, kf, wf, df, 4, 4, chunks, lambda j: [(j, 2 + j), (14 - j, 16 - j)])

        for z in range(5, 11):
            for t in range(4):
                cut = pl.ds(8, 32)
                sf[z, t, cut, :] += 0.5 * wf[4, z, t, cut, :]

        def residual(z, box):
            cut = pl.ds(16, 16)
            for t in range(4):
                here = sf[z, t, cut, :]
                scaled = gf[0, z, t, cut, :] - here + kf[z, t, cut, :] * (box[t] - here)
                plain = scaled * jf[z - 6, t]
                gf[cycle + 1, z, t, cut, :] = scaled
                tmp_r[z - 6, t, pl.ds(0, 16), :] = plain
                out = pl.ds(t * LANES, LANES)
                sol_out[z - 6, :, out] = here
                res_out[z - 6, :, out] = scaled

        sweep(sf, 6, 10, 4, 16, 16, residual)
        sent(last)
        return carry

    lax.fori_loop(0, CYCLES, cycle_body, 0)
    assert len(once) <= ONCE and len(every) <= EVERY


ONCE, EVERY = 80, 48


def shards(right_side, scale_field, mass_field, degrees, lower_bound, upper_bound):
    vmem = lambda *dims: pltpu.VMEM(dims, f32)
    fine, mid, low = (16, 4, 48, LANES), (14, 2, 40, LANES), (13, 1, 40, LANES)
    block = jax.ShapeDtypeStruct(right_side.shape, f32)
    whole = pl.BlockSpec(memory_space=pltpu.VMEM)
    scalar = pl.BlockSpec(memory_space=pltpu.SMEM)
    weighted, scaled = pl.pallas_call(
        kernel,
        out_shape=(block, block),
        in_specs=[pl.BlockSpec(memory_space=pl.ANY)] * 3 + [scalar] * 3,
        out_specs=(whole, whole),
        scratch_shapes=[
            vmem(4, 16, 512), vmem(4, 16, 512), vmem(4, 16, 512),
            vmem(4, *fine), vmem(*fine), vmem(*fine), vmem(5, *fine), vmem(5, *fine), vmem(*fine),
            vmem(4, 4, 40, LANES), vmem(4, 4, 16, LANES), vmem(4, 4, 24, LANES), vmem(4, 4, 24, LANES), vmem(4, 4, 24, LANES),
            vmem(3, *mid), vmem(*mid), vmem(*mid), vmem(5, *mid), vmem(5, *mid),
            vmem(3, 2, 24, LANES), vmem(2, 2, 8, LANES),
            vmem(6, 13, 5, 4, LANES), vmem(*low), vmem(*low), vmem(*low), vmem(5, *low), vmem(5, *low),
            vmem(8, LANES),
            vmem(3, MAXDEG, 2, 8, LANES),
            pltpu.SemaphoreType.DMA((3,)),
            pltpu.SemaphoreType.DMA((ONCE,)), pltpu.SemaphoreType.DMA((ONCE,)),
            pltpu.SemaphoreType.DMA((CYCLES, EVERY)), pltpu.SemaphoreType.DMA((CYCLES, EVERY)),
        ],
        compiler_params=pltpu.CompilerParams(
            collective_id=0, has_side_effects=True, vmem_limit_bytes=56 * 1024 * 1024
        ),
    )(right_side, scale_field, mass_field, degrees, lower_bound, upper_bound)
    inverse = 1.0 / scale_field
    return weighted * inverse, scaled * (scale_field + mass_field * inverse)


def solution(mesh):
    cut = P("slab", "level", None)
    return jax.shard_map(
        shards, mesh=mesh, in_specs=(cut, cut, cut, P(), P(), P()), out_specs=(cut, cut), check_vma=False
    )
```
